256 devices in a mesh: cfg: 2 (over core), vocab: 64 (over y, x, z_lo), rows: 2 (over z_hi).
Axes of the slice: x: 4, y: 4, z: 8 (z_hi: 2, z_lo: 4; z = z_hi * 4 + z_lo), core: 2. Of those that a mesh axis runs over, the one named last changes fastest.
Arguments:
- hidden: bfloat16 [2, 1024, 8192], P('cfg', None, ('rows', 'vocab')), may hold values from -72 to 72, as said below
- head: bfloat16 [8192, 65536], P('rows', 'vocab'), may hold values from -0.0625 to 0.0625
- scale_index: int32 [1024], P('rows'), may hold values from 0 to 8
- threshold: int32 [1024], P('rows'), may hold values from 2 to 33
Outputs:
- logprob: bfloat16 [1024, 65536], P(('rows', 'cfg'), 'vocab')
- typical: bfloat16 [1024, 65536], P(('rows', 'cfg'), 'vocab')
- entropy: float32 [1024], P(('rows', 'cfg'))
The draws below stay inside these ranges and needn't reach their ends.
Inputs may be any that keep to these rules, and one draw needn't show every extreme that they name: `hidden`: each entry is a normal value clipped to 6 scales and multiplied by a per-row factor between 1 and 12 (1 in some draws).
All inputs are finite; a program needn't handle non-finite values.
Results may differ from the reference program's by a relative error of at most 0.001.
Values may be sent and summed in bfloat16 or wider, within the bound.
No kernel may reach another device: no remote copies, remote signals or barrier semaphores. Data moves between devices by JAX's collectives and lax.ppermute only.
A program may use at most 64 MiB of HBM per device.

```python
import jax
import jax.numpy as jnp

D = 8192
V = 65536
ROWS = 1024


def draw_hidden(key, part):
    key = jax.random.fold_in(key, 11)
    first = jax.random.fold_in(key, 0)
    values = jnp.clip(jax.random.normal(first, (2, ROWS, D), jnp.float32), -6.0, 6.0)
    return values.astype(jnp.bfloat16)


def plant(drawn, key, smallest, largest):
    index_at = [jax.random.randint(jax.random.fold_in(key, axis), (), 0, length) for axis, length in enumerate(drawn.shape)]
    main_axis = drawn.shape.index(max(drawn.shape))
    neighbour = index_at[:main_axis] + [(index_at[main_axis] + 1) % drawn.shape[main_axis]] + index_at[main_axis + 1:]
    return drawn.at[tuple(index_at)].set(smallest).at[tuple(neighbour)].set(largest)


def block_scale(rng, shape, cuts, low, top_value):
    gain, own = 1.0, jax.random.fold_in(rng, 6)
    for axis_at, shards_of in cuts:
        heights = jnp.exp(jax.random.uniform(jax.random.fold_in(own, axis_at), (shards_of,), jnp.float32, low / len(cuts), top_value / len(cuts)))
        gain = gain * jnp.repeat(heights, shape[axis_at] // shards_of).reshape([-1 if axis == axis_at else 1 for axis in range(len(shape))])
    return gain


def bell_draw(key, extent, width, reach, cuts=(), kind=jnp.bfloat16):
    values = jax.random.normal(key, extent, jnp.float32) * width
    if len(cuts) > 0:
        values = block_scale(key, extent, cuts, -0.22, 0.18) * values
    return jnp.clip(values, min=-reach, max=reach).astype(kind)


def setup_inputs(seed: int = 0) -> dict:
    streams_of = jax.random.split(jax.random.key(seed), 5)
    return {
        "hidden": draw_hidden(jax.random.fold_in(streams_of[4], 71), 0),
        "head": bell_draw(streams_of[1], (D, V), D ** -0.5, 0.0625, ((0, 2), (1, 64))),
        "scale_index": plant(jax.random.randint(streams_of[2], (ROWS,), 0, 9), jax.random.fold_in(streams_of[2], 1), 0, 8).astype(jnp.int32),
        "threshold": plant(jax.random.randint(streams_of[3], (ROWS,), 2, 34), jax.random.fold_in(streams_of[3], 1), 2, 33).astype(jnp.int32),
    }


def reference(hidden, head, scale_index, threshold):
    conditional = jnp.dot(hidden[0], head, preferred_element_type=jnp.float32)
    unconditional = jnp.dot(hidden[1], head, preferred_element_type=jnp.float32)
    guide = 1.0 + 0.5 * scale_index.astype(jnp.float32)
    limits = threshold.astype(jnp.float32) / 8.0
    guided = unconditional + guide[:, None] * (conditional - unconditional)
    peak = jnp.max(guided, axis=1)
    expo = jnp.exp(guided - peak[:, None])
    total = jnp.sum(expo, axis=1)
    moment = jnp.sum(expo * guided, axis=1)
    lse = peak + jnp.log(total)
    entropy = lse - moment / total
    shifted = guided - lse[:, None]
    deviation = -shifted - entropy[:, None]
    typical = jax.nn.sigmoid(2.0 * (limits[:, None] - jnp.abs(deviation)))
    return shifted.astype(jnp.bfloat16), typical.astype(jnp.bfloat16), entropy
```

```python
import math

import jax
import jax.numpy as jnp
from jax import lax
from jax.experimental import pallas as pl
from jax.experimental.pallas import tpu as pltpu
from jax.sharding import Mesh, PartitionSpec as P

AXES = ("cfg", "y", "x", "zl", "zh")
SIZES = (2, 4, 4, 4, 2)
TOP = 32767.0
STEP = math.log(2.0) / 256.0


def pairs(axes, move):
    dims = [SIZES[AXES.index(a)] for a in axes]
    route = []
    for i in range(math.prod(dims)):
        rest, at = i, {}
        for a, n in reversed(list(zip(axes, dims))):
            at[a], rest = rest % n, rest // n
        to = move(dict(at))
        j = 0
        for a, n in zip(axes, dims):
            j = j * n + to[a] % n
        route.append((i, j))
    return route


def shifted(block, axis, k):
    return lax.ppermute(block, axis, pairs((axis,), lambda at: {axis: at[axis] + k}))


def crossed(block, first, second, k):
    def move(at):
        along = first if at["cfg"] == 0 else second
        at[along] += k
        return at

    axes = ("cfg", "y", "x")
    return lax.ppermute(block, axes, pairs(axes, move))


def code_of(largest):
    return jnp.ceil(jnp.log(jnp.maximum(largest, 1e-30)) * (1.0 / STEP)) + 1.0


def scale_of(code):
    return jnp.exp(code * STEP) * (1.0 / TOP)


def coded(values, scale):
    return jnp.clip(jnp.round(values / scale), -TOP, TOP).astype(jnp.int32).astype(jnp.int16)


def mix_kernel(core_ref, own_ref, other_ref, guide_ref, out_ref):
    own = own_ref[...].astype(jnp.float32)
    other = other_ref[...].astype(jnp.float32)
    first = core_ref[0] == 0
    cond = jnp.where(first, own, other)
    uncond = jnp.where(first, other, own)
    mixed = uncond + guide_ref[...] * (cond - uncond)
    code = code_of(jnp.max(jnp.abs(mixed), axis=0, keepdims=True))
    out_ref[:64] = coded(mixed, scale_of(code))
    out_ref[64:] = jnp.broadcast_to(code, (16, code.shape[1])).astype(jnp.int32).astype(jnp.int16)


def mix(core, own, other, guide):
    width = own.shape[1]
    return pl.pallas_call(
        mix_kernel,
        out_shape=jax.ShapeDtypeStruct((80, width), jnp.int16),
        in_specs=[pl.BlockSpec(memory_space=pltpu.SMEM)] + [pl.BlockSpec(memory_space=pltpu.VMEM)] * 3,
        out_specs=pl.BlockSpec(memory_space=pltpu.VMEM),
        name="mix",
    )(core, own, other, guide)


def stack_kernel(place_ref, a_ref, b_ref, c_ref, d_ref, out_ref):
    width = a_ref.shape[1]
    row = lax.broadcasted_iota(jnp.int32, (16, width), 0)
    codes = jnp.zeros((16, width), jnp.int32)
    for k, ref in enumerate((a_ref, b_ref, c_ref, d_ref)):
        place = place_ref[k]
        out_ref[pl.ds(pl.multiple_of(place * 64, 64), 64), :] = ref[:64]
        codes = jnp.where(row == place, ref[64:].astype(jnp.int32), codes)
    out_ref[256:] = codes.astype(jnp.int16)


def stack(place, parts):
    width = parts[0].shape[1]
    return pl.pallas_call(
        stack_kernel,
        out_shape=jax.ShapeDtypeStruct((272, width), jnp.int16),
        in_specs=[pl.BlockSpec(memory_space=pltpu.SMEM)] + [pl.BlockSpec(memory_space=pltpu.VMEM)] * 4,
        out_specs=pl.BlockSpec(memory_space=pltpu.VMEM),
        name="stack",
    )(place, *parts)


def product_kernel(index_ref, head_ref, *refs):
    parts, out_ref, total_ref = refs[:4], refs[4], refs[5]
    step = pl.program_id(0)

    @pl.when(step == 0)
    def _():
        total_ref[...] = jnp.zeros_like(total_ref)

    for k, part in enumerate(parts):

        @pl.when(step // 4 == k)
        def _(part=part):
            scale = scale_of(part[256:].astype(jnp.float32))
            high, low = [], []
            for j in range(4):
                value = part[64 * j : 64 * j + 64].astype(jnp.float32) * scale[j : j + 1]
                top = value.astype(jnp.bfloat16)
                high.append(top)
                low.append((value - top.astype(jnp.float32)).astype(jnp.bfloat16))
            weight = head_ref[...]
            dims = (((0,), (0,)), ((), ()))
            total_ref[...] += lax.dot_general(
                jnp.concatenate(high, 0), weight, dims, preferred_element_type=jnp.float32
            ) + lax.dot_general(jnp.concatenate(low, 0), weight, dims, preferred_element_type=jnp.float32)

    @pl.when(step == 15)
    def _():
        if out_ref.dtype == jnp.float32:
            out_ref[...] = total_ref[...]
        else:
            total = total_ref[...]
            count = total.shape[0]
            code = code_of(jnp.max(jnp.abs(total), axis=1, keepdims=True))
            out_ref[:count] = coded(total, scale_of(code))
            across = jnp.transpose(jnp.broadcast_to(code, (count, 128)))[:16]
            out_ref[count:, :count] = across.astype(jnp.int32).astype(jnp.int16)


def product(index, head, parts, keep):
    tokens, width = parts[0].shape[1], head.shape[1]

    def block(k):
        return lambda s, index: (jnp.clip(s - 4 * k, 0, 3), 0)

    out = (
        jax.ShapeDtypeStruct((tokens, width), jnp.float32)
        if keep
        else jax.ShapeDtypeStruct((tokens + 16, width), jnp.int16)
    )
    return pl.pallas_call(
        product_kernel,
        out_shape=out,
        grid_spec=pltpu.PrefetchScalarGridSpec(
            num_scalar_prefetch=1,
            grid=(16,),
            in_specs=[pl.BlockSpec((256, width), lambda s, index: (index[s], 0))]
            + [pl.BlockSpec((272, tokens), block(k)) for k in range(4)],
            out_specs=pl.BlockSpec(out.shape, lambda s, index: (0, 0)),
            scratch_shapes=[pltpu.VMEM((tokens, width), jnp.float32)],
        ),
        compiler_params=pltpu.CompilerParams(vmem_limit_bytes=24 << 20),
        cost_estimate=pl.CostEstimate(
            flops=4 * tokens * 4096 * width, bytes_accessed=10 << 20, transcendentals=0
        ),
        name="product",
    )(index, head, *parts)


def merged(stats):
    peak = stats[0][0]
    for s in stats[1:]:
        peak = jnp.maximum(peak, s[0])
    total = moment = 0.0
    for s in stats:
        weight = jnp.exp(s[0] - peak)
        total += s[1] * weight
        moment += s[2] * weight
    return jnp.stack([peak, total, moment])


def local(hidden, head, scale_index, threshold):
    core, far = lax.axis_index("cfg"), lax.axis_index("zh")
    y, x, zl = lax.axis_index("y"), lax.axis_index("x"), lax.axis_index("zl")
    features = hidden[0].T

    def tokens_of(which):
        cut = [
            lax.dynamic_slice_in_dim(features, half * 512 + which * 256, 256, 1) for half in (1 - far, far)
        ]
        return jnp.concatenate(cut, 1)

    other = lax.ppermute(tokens_of(1 - core), "cfg", [(0, 1), (1, 0)])
    guide = 1.0 + 0.5 * lax.dynamic_slice_in_dim(scale_index, core * 256, 256, 0).astype(jnp.float32)
    limits = lax.dynamic_slice_in_dim(threshold, core * 256, 256, 0).astype(jnp.float32) / 8.0
    away_guide = lax.ppermute(guide, "zh", [(0, 1), (1, 0)])
    guides = jnp.concatenate([away_guide, guide])[None]

    mixed = mix(core[None], tokens_of(core), other, guides)
    near = [mixed] + [shifted(mixed, "zl", k) for k in (1, 2, 3)]
    place = jnp.stack([(zl - k) % 4 for k in range(4)])
    column = stack(place, near)

    line = [column] + [crossed(column, "x", "y", k) for k in (1, 2, 3)]
    index = []
    for k2 in range(4):
        for k1 in range(4):
            a = jnp.where(core == 0, y - k2, y - k1) % 4
            b = jnp.where(core == 0, x - k1, x - k2) % 4
            index.append(a * 4 + b)
    index = jnp.stack(index).astype(jnp.int32)

    def gathered(cut, after):
        block = jnp.concatenate([p[:, cut] for p in line], 0)
        if after is not None:
            block = lax.optimization_barrier((block, *after))[0]
        return [block] + [crossed(block, "y", "x", k) for k in (1, 2, 3)]

    away_parts = gathered(slice(0, 256), None)
    sent = product(index, head, away_parts, False)
    back = lax.ppermute(sent, "zh", [(0, 1), (1, 0)])
    home_parts = gathered(slice(256, 512), away_parts[1:])
    kept = product(index, head, home_parts, True)

    scale = scale_of(back[256, :256].astype(jnp.float32))
    guided = kept + back[:256].astype(jnp.float32) * scale[:, None]
    peak = jnp.max(guided, axis=1)
    expo = jnp.exp(guided - peak[:, None])
    stats = jnp.stack([peak, jnp.sum(expo, axis=1), jnp.sum(expo * guided, axis=1)])
    for axis in ("zl", "x", "y"):
        stats = merged([stats] + [shifted(stats, axis, k) for k in (1, 2, 3)])
    lse = stats[0] + jnp.log(stats[1])
    entropy = lse - stats[2] / stats[1]
    logprob = guided - lse[:, None]
    deviation = -logprob - entropy[:, None]
    typical = jax.nn.sigmoid(2.0 * (limits[:, None] - jnp.abs(deviation)))
    return logprob.astype(jnp.bfloat16), typical.astype(jnp.bfloat16), entropy


def solution(mesh):
    torus = Mesh(mesh.devices.reshape(SIZES), AXES)
    vocab = ("y", "x", "zl")
    return jax.shard_map(
        local,
        mesh=torus,
        in_specs=(P("cfg", None, ("zh", *vocab)), P("zh", vocab), P("zh"), P("zh")),
        out_specs=(P(("zh", "cfg"), vocab), P(("zh", "cfg"), vocab), P(("zh", "cfg"))),
        check_vma=False,
    )
```

```python
import math

import jax
import jax.numpy as jnp
from jax import lax
from jax.experimental import pallas as pl
from jax.experimental.pallas import tpu as pltpu
from jax.sharding import Mesh, PartitionSpec as P

AXES = ("cfg", "y", "x", "zl", "zh")
SIZES = (2, 4, 4, 4, 2)
TOP = 32767.0
STEP = math.log(2.0) / 256.0


def pairs(axes, move):
    dims = [SIZES[AXES.index(a)] for a in axes]
    route = []
    for i in range(math.prod(dims)):
        rest, at = i, {}
        for a, n in reversed(list(zip(axes, dims))):
            at[a], rest = rest % n, rest // n
        to = move(dict(at))
        j = 0
        for a, n in zip(axes, dims):
            j = j * n + to[a] % n
        route.append((i, j))
    return route


def shifted(block, axis, k):
    return lax.ppermute(block, axis, pairs((axis,), lambda at: {axis: at[axis] + k}))


def crossed(block, first, second, k):
    def move(at):
        along = first if at["cfg"] == 0 else second
        at[along] += k
        return at

    axes = ("cfg", "y", "x")
    return lax.ppermute(block, axes, pairs(axes, move))


def code_of(largest):
    return jnp.ceil(jnp.log(jnp.maximum(largest, 1e-30)) * (1.0 / STEP)) + 1.0


def scale_of(code):
    return jnp.exp(code * STEP) * (1.0 / TOP)


def coded(values, scale):
    return jnp.clip(jnp.round(values / scale), -TOP, TOP).astype(jnp.int32).astype(jnp.int16)


def in_vmem(count):
    return [pl.BlockSpec(memory_space=pltpu.VMEM)] * count


def room(mib):
    return pltpu.CompilerParams(vmem_limit_bytes=mib << 20)


def load_kernel(*refs):
    count = len(refs) // 2
    loads = [pltpu.make_async_copy(refs[i], refs[count + i], refs[-1].at[i]) for i in range(count)]
    for load in loads:
        load.start()
    for load in loads:
        load.wait()


def load(*arrays):
    return pl.pallas_call(
        load_kernel,
        out_shape=[jax.ShapeDtypeStruct(a.shape, a.dtype) for a in arrays],
        in_specs=[pl.BlockSpec(memory_space=pl.ANY)] * len(arrays),
        out_specs=in_vmem(len(arrays)),
        scratch_shapes=[pltpu.SemaphoreType.DMA((len(arrays),))],
        compiler_params=room(50),
        cost_estimate=pl.CostEstimate(flops=0, bytes_accessed=16 << 20, transcendentals=0),
        name="load",
    )(*arrays)


def mix_kernel(place_ref, own_ref, other_ref, own_scale_ref, away_scale_ref, out_ref):
    core, far = place_ref[0], place_ref[1]
    first = core == 0
    for n, half in enumerate((1 - far, far)):
        cut = pl.ds(pl.multiple_of(half * 512 + core * 256, 256), 256)
        scale_ref = away_scale_ref if n == 0 else own_scale_ref
        scales = scale_ref[:, pl.ds(pl.multiple_of(core * 256, 256), 256)]
        guide = 1.0 + 0.5 * scales.astype(jnp.float32)
        own = own_ref[:, cut].astype(jnp.float32)
        other = other_ref[:, cut].astype(jnp.float32)
        cond = jnp.where(first, own, other)
        uncond = jnp.where(first, other, own)
        mixed = uncond + guide * (cond - uncond)
        code = code_of(jnp.max(jnp.abs(mixed), axis=0, keepdims=True))
        at = slice(256 * n, 256 * n + 256)
        out_ref[:64, at] = coded(mixed, scale_of(code))
        out_ref[64:, at] = jnp.broadcast_to(code, (16, 256)).astype(jnp.int32).astype(jnp.int16)


def mix(place, own, other, own_scale, away_scale):
    return pl.pallas_call(
        mix_kernel,
        out_shape=jax.ShapeDtypeStruct((80, 512), jnp.int16),
        in_specs=[pl.BlockSpec(memory_space=pltpu.SMEM)] + in_vmem(4),
        out_specs=in_vmem(1)[0],
        compiler_params=room(4),
        name="mix",
    )(place, own, other, own_scale, away_scale)


def stack_kernel(place_ref, a_ref, b_ref, c_ref, d_ref, *out_refs):
    row = lax.broadcasted_iota(jnp.int32, (16, 256), 0)
    for n, out_ref in enumerate(out_refs):
        at = slice(256 * n, 256 * n + 256)
        codes = jnp.zeros((16, 256), jnp.int32)
        for k, ref in enumerate((a_ref, b_ref, c_ref, d_ref)):
            place = place_ref[k]
            out_ref[pl.ds(pl.multiple_of(place * 64, 64), 64), :] = ref[:64, at]
            codes = jnp.where(row == place, ref[64:, at].astype(jnp.int32), codes)
        out_ref[256:] = codes.astype(jnp.int16)


def stack(place, parts):
    return pl.pallas_call(
        stack_kernel,
        out_shape=[jax.ShapeDtypeStruct((272, 256), jnp.int16)] * 2,
        in_specs=[pl.BlockSpec(memory_space=pltpu.SMEM)] + in_vmem(4),
        out_specs=in_vmem(2),
        compiler_params=room(4),
        name="stack",
    )(place, *parts)


def product_kernel(index_ref, head_ref, *refs):
    parts, out_ref, total_ref = refs[:4], refs[4], refs[5]
    count = total_ref.shape[0] // 2
    dims = (((0,), (0,)), ((), ()))
    for k, part in enumerate(parts):
        total = None
        for piece in range(4):
            base = 272 * piece
            scale = scale_of(part[base + 256 : base + 272].astype(jnp.float32))
            high, low = [], []
            for j in range(4):
                values = part[base + 64 * j : base + 64 * j + 64].astype(jnp.float32) * scale[j : j + 1]
                top = values.astype(jnp.bfloat16)
                high.append(top)
                low.append((values - top.astype(jnp.float32)).astype(jnp.bfloat16))
            both = jnp.concatenate([jnp.concatenate(high, 0), jnp.concatenate(low, 0)], 1)
            weight = head_ref[pl.ds(pl.multiple_of(index_ref[4 * k + piece] * 256, 256), 256), :]
            term = lax.dot_general(both, weight, dims, preferred_element_type=jnp.float32)
            total = term if total is None else total + term
        if k == 0:
            total_ref[...] = total
        else:
            total_ref[...] += total
    total = total_ref[:count] + total_ref[count:]
    if out_ref.dtype == jnp.float32:
        out_ref[...] = total
    else:
        code = code_of(jnp.max(jnp.abs(total), axis=1, keepdims=True))
        out_ref[:count] = coded(total, scale_of(code))
        across = jnp.transpose(jnp.broadcast_to(code, (count, 128)))[:16]
        out_ref[count:] = jnp.zeros((16, total.shape[1]), jnp.int16)
        out_ref[count:, :count] = across.astype(jnp.int32).astype(jnp.int16)


def product(index, head, parts, keep):
    tokens, width = parts[0].shape[1], head.shape[1]
    out = (
        jax.ShapeDtypeStruct((tokens, width), jnp.float32)
        if keep
        else jax.ShapeDtypeStruct((tokens + 16, width), jnp.int16)
    )
    return pl.pallas_call(
        product_kernel,
        out_shape=out,
        in_specs=[pl.BlockSpec(memory_space=pltpu.SMEM)] + in_vmem(5),
        out_specs=in_vmem(1)[0],
        scratch_shapes=[pltpu.VMEM((2 * tokens, width), jnp.float32)],
        compiler_params=room(24),
        cost_estimate=pl.CostEstimate(
            flops=4 * tokens * 4096 * width, bytes_accessed=10 << 20, transcendentals=0
        ),
        name="product",
    )(index, head, *parts)


def join_kernel(kept_ref, back_ref, guided_ref, stats_ref):
    count = kept_ref.shape[0]
    codes = back_ref[count:, :count].astype(jnp.float32)[:1]
    scale = jnp.transpose(jnp.broadcast_to(scale_of(codes), (128, count)))[:, :1]
    guided = kept_ref[...] + back_ref[:count].astype(jnp.float32) * scale
    peak = jnp.max(guided, axis=1, keepdims=True)
    expo = jnp.exp(guided - peak)
    total = jnp.sum(expo, axis=1, keepdims=True)
    moment = jnp.sum(expo * guided, axis=1, keepdims=True)
    lane = lax.broadcasted_iota(jnp.int32, (count, 128), 1)
    table = jnp.where(lane == 0, peak, jnp.where(lane == 1, total, moment))
    stats_ref[...] = jnp.transpose(table)[:8]
    guided_ref[...] = guided


def join(kept, back):
    return pl.pallas_call(
        join_kernel,
        out_shape=(
            jax.ShapeDtypeStruct(kept.shape, jnp.float32),
            jax.ShapeDtypeStruct((8, kept.shape[0]), jnp.float32),
        ),
        in_specs=in_vmem(2),
        out_specs=in_vmem(2),
        compiler_params=room(12),
        name="join",
    )(kept, back)


def merged(stats):
    peak = stats[0][:1]
    for s in stats[1:]:
        peak = jnp.maximum(peak, s[:1])
    total = moment = 0.0
    for s in stats:
        weight = jnp.exp(s[:1] - peak)
        total += s[1:2] * weight
        moment += s[2:3] * weight
    return jnp.concatenate([peak, total, moment, stats[0][3:]])


def local(hidden, head, scale_index, threshold):
    core, far = lax.axis_index("cfg"), lax.axis_index("zh")
    y, x, zl = lax.axis_index("y"), lax.axis_index("x"), lax.axis_index("zl")
    features = hidden[0].T
    other = lax.ppermute(features, "cfg", [(0, 1), (1, 0)])
    away_scale = lax.ppermute(scale_index, "zh", [(0, 1), (1, 0)])
    limits = lax.dynamic_slice_in_dim(threshold, core * 256, 256, 0).astype(jnp.float32) / 8.0

    head, own, own_scale = load(head, features, scale_index[None])
    mixed = mix(jnp.stack([core, far]), own, other, own_scale, away_scale[None])
    mixed, head = lax.optimization_barrier((mixed, head))
    near = [mixed] + [shifted(mixed, "zl", k) for k in (1, 2, 3)]
    place = jnp.stack([(zl - k) % 4 for k in range(4)])
    away_column, home_column = stack(place, near)

    index = []
    for k2 in range(4):
        for k1 in range(4):
            a = jnp.where(core == 0, y - k2, y - k1) % 4
            b = jnp.where(core == 0, x - k1, x - k2) % 4
            index.append(a * 4 + b)
    index = jnp.stack(index).astype(jnp.int32)

    def spread(block, first, second):
        return [block] + [crossed(block, first, second, k) for k in (1, 2, 3)]

    away_line = spread(away_column, "x", "y")
    away_parts = spread(jnp.concatenate(away_line, 0), "y", "x")
    home_column = lax.optimization_barrier((home_column, *away_line))[0]
    home_line = spread(home_column, "x", "y")
    sent = product(index, head, away_parts, False)
    home_block = jnp.concatenate(home_line, 0)
    home_block = lax.optimization_barrier((home_block, *away_parts))[0]
    home_parts = spread(home_block, "y", "x")
    back = lax.ppermute(sent, "zh", [(0, 1), (1, 0)])
    kept = product(index, head, home_parts, True)

    guided, stats = join(kept, back)
    for axis in ("zl", "x", "y"):
        stats = merged([stats] + [shifted(stats, axis, k) for k in (1, 2, 3)])
    lse = stats[0] + jnp.log(stats[1])
    entropy = lse - stats[2] / stats[1]
    logprob = guided - lse[:, None]
    deviation = -logprob - entropy[:, None]
    typical = jax.nn.sigmoid(2.0 * (limits[:, None] - jnp.abs(deviation)))
    return logprob.astype(jnp.bfloat16), typical.astype(jnp.bfloat16), entropy


def solution(mesh):
    torus = Mesh(mesh.devices.reshape(SIZES), AXES)
    vocab = ("y", "x", "zl")
    return jax.shard_map(
        local,
        mesh=torus,
        in_specs=(P("cfg", None, ("zh", *vocab)), P("zh", vocab), P("zh"), P("zh")),
        out_specs=(P(("zh", "cfg"), vocab), P(("zh", "cfg"), vocab), P(("zh", "cfg"))),
        check_vma=False,
    )
```

```python
import math

import jax
import jax.numpy as jnp
from jax import lax
from jax.experimental import pallas as pl
from jax.experimental.pallas import tpu as pltpu
from jax.sharding import Mesh, PartitionSpec as P

AXES = ("cfg", "y", "x", "zl", "zh")
SIZES = (2, 4, 4, 4, 2)
TOP = 32767.0
CHUNKS = ((0, 256), (256, 256))
STEP = math.log(2.0) / 256.0


def pairs(axes, move):
    dims = [SIZES[AXES.index(a)] for a in axes]
    route = []
    for i in range(math.prod(dims)):
        rest, at = i, {}
        for a, n in reversed(list(zip(axes, dims))):
            at[a], rest = rest % n, rest // n
        to = move(dict(at))
        j = 0
        for a, n in zip(axes, dims):
            j = j * n + to[a] % n
        route.append((i, j))
    return route


def shifted(block, axis, k):
    return lax.ppermute(block, axis, pairs((axis,), lambda at: {axis: at[axis] + k}))


def crossed(block, first, second, k):
    def move(at):
        along = first if at["cfg"] == 0 else second
        at[along] += k
        return at

    axes = ("cfg", "y", "x")
    return lax.ppermute(block, axes, pairs(axes, move))


def code_of(largest):
    return jnp.ceil(jnp.log(jnp.maximum(largest, 1e-30)) * (1.0 / STEP)) + 1.0


def scale_of(code):
    return jnp.exp(code * STEP) * (1.0 / TOP)


def coded(values, scale):
    return jnp.clip(jnp.round(values / scale), -TOP, TOP).astype(jnp.int32).astype(jnp.int16)


def in_vmem(count):
    return [pl.BlockSpec(memory_space=pltpu.VMEM)] * count


def room(mib):
    return pltpu.CompilerParams(vmem_limit_bytes=mib << 20)


def load_kernel(*refs):
    count = len(refs) // 2
    loads = [pltpu.make_async_copy(refs[i], refs[count + i], refs[-1].at[i]) for i in range(count)]
    for load in loads:
        load.start()
    for load in loads:
        load.wait()


def load(*arrays):
    return pl.pallas_call(
        load_kernel,
        out_shape=[jax.ShapeDtypeStruct(a.shape, a.dtype) for a in arrays],
        in_specs=[pl.BlockSpec(memory_space=pl.ANY)] * len(arrays),
        out_specs=in_vmem(len(arrays)),
        scratch_shapes=[pltpu.SemaphoreType.DMA((len(arrays),))],
        compiler_params=room(44),
        cost_estimate=pl.CostEstimate(flops=0, bytes_accessed=16 << 20, transcendentals=0),
        name="load",
    )(*arrays)


def mix_kernel(place_ref, own_ref, other_ref, own_scale_ref, away_scale_ref, out_ref):
    core, far = place_ref[0], place_ref[1]
    first = core == 0
    for n, half in enumerate((1 - far, far)):
        cut = pl.ds(pl.multiple_of(half * 512 + core * 256, 256), 256)
        scale_ref = away_scale_ref if n == 0 else own_scale_ref
        scales = scale_ref[:, pl.ds(pl.multiple_of(core * 256, 256), 256)]
        guide = 1.0 + 0.5 * scales.astype(jnp.float32)
        own = own_ref[:, cut].astype(jnp.float32)
        other = other_ref[:, cut].astype(jnp.float32)
        cond = jnp.where(first, own, other)
        uncond = jnp.where(first, other, own)
        mixed = uncond + guide * (cond - uncond)
        code = code_of(jnp.max(jnp.abs(mixed), axis=0, keepdims=True))
        at = slice(256 * n, 256 * n + 256)
        out_ref[:64, at] = coded(mixed, scale_of(code))
        out_ref[64:, at] = jnp.broadcast_to(code, (16, 256)).astype(jnp.int32).astype(jnp.int16)


def mix(place, own, other, own_scale, away_scale):
    return pl.pallas_call(
        mix_kernel,
        out_shape=jax.ShapeDtypeStruct((80, 512), jnp.int16),
        in_specs=[pl.BlockSpec(memory_space=pltpu.SMEM)] + in_vmem(4),
        out_specs=in_vmem(1)[0],
        compiler_params=room(4),
        name="mix",
    )(place, own, other, own_scale, away_scale)


def stack_kernel(place_ref, a_ref, b_ref, c_ref, d_ref, out_ref):
    width = a_ref.shape[1]
    row = lax.broadcasted_iota(jnp.int32, (16, width), 0)
    codes = jnp.zeros((16, width), jnp.int32)
    for k, ref in enumerate((a_ref, b_ref, c_ref, d_ref)):
        place = place_ref[k]
        out_ref[pl.ds(pl.multiple_of(place * 64, 64), 64), :] = ref[:64]
        codes = jnp.where(row == place, ref[64:].astype(jnp.int32), codes)
    out_ref[256:] = codes.astype(jnp.int16)


def stack(place, parts):
    return pl.pallas_call(
        stack_kernel,
        out_shape=jax.ShapeDtypeStruct((272, parts[0].shape[1]), jnp.int16),
        in_specs=[pl.BlockSpec(memory_space=pltpu.SMEM)] + in_vmem(4),
        out_specs=in_vmem(1)[0],
        compiler_params=room(4),
        name="stack",
    )(place, *parts)


def product_kernel(index_ref, head_ref, *refs):
    parts, out_ref, total_ref = refs[:4], refs[4], refs[5]
    count = total_ref.shape[0] // 2
    dims = (((0,), (0,)), ((), ()))
    for k, part in enumerate(parts):
        total = None
        for piece in range(4):
            base = 272 * piece
            scale = scale_of(part[base + 256 : base + 272].astype(jnp.float32))
            high, low = [], []
            for j in range(4):
                values = part[base + 64 * j : base + 64 * j + 64].astype(jnp.float32) * scale[j : j + 1]
                top = values.astype(jnp.bfloat16)
                high.append(top)
                low.append((values - top.astype(jnp.float32)).astype(jnp.bfloat16))
            both = jnp.concatenate([jnp.concatenate(high, 0), jnp.concatenate(low, 0)], 1)
            weight = head_ref[pl.ds(pl.multiple_of(index_ref[4 * k + piece] * 256, 256), 256), :]
            term = lax.dot_general(both, weight, dims, preferred_element_type=jnp.float32)
            total = term if total is None else total + term
        if k == 0:
            total_ref[...] = total
        else:
            total_ref[...] += total
    total = total_ref[:count] + total_ref[count:]
    if out_ref.dtype == jnp.float32:
        out_ref[...] = total
    else:
        code = code_of(jnp.max(jnp.abs(total), axis=1, keepdims=True))
        out_ref[:count] = coded(total, scale_of(code))
        across = jnp.transpose(jnp.broadcast_to(code, (count, 128)))[:16]
        out_ref[count:] = jnp.zeros((16, total.shape[1]), jnp.int16)
        out_ref[count:, :count] = across.astype(jnp.int32).astype(jnp.int16)


def product(index, head, parts, keep):
    tokens, width = parts[0].shape[1], head.shape[1]
    out = (
        jax.ShapeDtypeStruct((tokens, width), jnp.float32)
        if keep
        else jax.ShapeDtypeStruct((tokens + 16, width), jnp.int16)
    )
    return pl.pallas_call(
        product_kernel,
        out_shape=out,
        in_specs=[pl.BlockSpec(memory_space=pltpu.SMEM)] + in_vmem(5),
        out_specs=in_vmem(1)[0],
        scratch_shapes=[pltpu.VMEM((2 * tokens, width), jnp.float32)],
        compiler_params=room(24),
        cost_estimate=pl.CostEstimate(
            flops=4 * tokens * 4096 * width, bytes_accessed=10 << 20, transcendentals=0
        ),
        name="product",
    )(index, head, *parts)


def join_kernel(kept_ref, *refs):
    backs, guided_ref, stats_ref = refs[:-2], refs[-2], refs[-1]
    start = 0
    for back_ref in backs:
        count = back_ref.shape[0] - 16
        rows = slice(start, start + count)
        codes = back_ref[count:, :count].astype(jnp.float32)[:1]
        scale = jnp.transpose(jnp.broadcast_to(scale_of(codes), (128, count)))[:, :1]
        guided = kept_ref[rows] + back_ref[:count].astype(jnp.float32) * scale
        peak = jnp.max(guided, axis=1, keepdims=True)
        expo = jnp.exp(guided - peak)
        total = jnp.sum(expo, axis=1, keepdims=True)
        moment = jnp.sum(expo * guided, axis=1, keepdims=True)
        lane = lax.broadcasted_iota(jnp.int32, (count, 128), 1)
        table = jnp.where(lane == 0, peak + jnp.log(total), moment / total)
        stats_ref[:, rows] = jnp.transpose(table)[:2]
        guided_ref[rows] = guided
        start += count


def join(kept, backs):
    return pl.pallas_call(
        join_kernel,
        out_shape=(
            jax.ShapeDtypeStruct(kept.shape, jnp.float32),
            jax.ShapeDtypeStruct((2, kept.shape[0]), jnp.float32),
        ),
        in_specs=in_vmem(1 + len(backs)),
        out_specs=in_vmem(2),
        compiler_params=room(12),
        name="join",
    )(kept, *backs)


def local(hidden, head, scale_index, threshold):
    core, far = lax.axis_index("cfg"), lax.axis_index("zh")
    y, x, zl = lax.axis_index("y"), lax.axis_index("x"), lax.axis_index("zl")
    features = hidden[0].T
    other = lax.ppermute(features, "cfg", [(0, 1), (1, 0)])
    away_scale = lax.ppermute(scale_index, "zh", [(0, 1), (1, 0)])
    limits = lax.dynamic_slice_in_dim(threshold, core * 256, 256, 0).astype(jnp.float32) / 8.0

    head, own, own_scale = load(head, features, scale_index[None])
    mixed = mix(jnp.stack([core, far]), own, other, own_scale, away_scale[None])
    mixed, head = lax.optimization_barrier((mixed, head))
    near = [mixed] + [shifted(mixed, "zl", k) for k in (1, 2, 3)]
    place = jnp.stack([(zl - k) % 4 for k in range(4)])
    column = stack(place, near)

    index = []
    for k2 in range(4):
        for k1 in range(4):
            a = jnp.where(core == 0, y - k2, y - k1) % 4
            b = jnp.where(core == 0, x - k1, x - k2) % 4
            index.append(a * 4 + b)
    index = jnp.stack(index).astype(jnp.int32)

    def spread(block, first, second):
        return [block] + [crossed(block, first, second, k) for k in (1, 2, 3)]

    line = spread(column, "x", "y")
    backs, before = [], ()
    for start, count in CHUNKS:
        block = jnp.concatenate([part[:, start : start + count] for part in line], 0)
        if start == 256:
            block = lax.optimization_barrier((block, *before))[0]
        before = spread(block, "y", "x")
        result = product(index, head, before, start >= 256)
        if start < 256:
            backs.append(lax.ppermute(result, "zh", [(0, 1), (1, 0)]))

    guided, stats = join(result, backs)
    stats = lax.all_to_all(jnp.broadcast_to(stats, (64, 2, 256)), ("y", "x", "zl"), 0, 0, tiled=True)
    each, mean = stats[:, 0], stats[:, 1]
    top = jnp.max(each, axis=0)
    weight = jnp.exp(each - top)
    total = jnp.sum(weight, axis=0)
    lse = top + jnp.log(total)
    entropy = lse - jnp.sum(weight * mean, axis=0) / total
    logprob = guided - lse[:, None]
    deviation = -logprob - entropy[:, None]
    typical = jax.nn.sigmoid(2.0 * (limits[:, None] - jnp.abs(deviation)))
    return logprob.astype(jnp.bfloat16), typical.astype(jnp.bfloat16), entropy


def solution(mesh):
    torus = Mesh(mesh.devices.reshape(SIZES), AXES)
    vocab = ("y", "x", "zl")
    return jax.shard_map(
        local,
        mesh=torus,
        in_specs=(P("cfg", None, ("zh", *vocab)), P("zh", vocab), P("zh"), P("zh")),
        out_specs=(P(("zh", "cfg"), vocab), P(("zh", "cfg"), vocab), P(("zh", "cfg"))),
        check_vma=False,
    )
```

```python
import functools
import math

import jax
import jax.numpy as jnp
from jax import lax
from jax.experimental import pallas as pl
from jax.experimental.pallas import tpu as pltpu
from jax.sharding import Mesh, PartitionSpec as P

AXES = ("cfg", "y", "x", "zl", "zh")
SIZES = (2, 4, 4, 4, 2)
TOP = 32767.0
CHUNKS = ((0, 128), (128, 128), (256, 256))
STEP = math.log(2.0) / 256.0


def pairs(axes, move):
    dims = [SIZES[AXES.index(a)] for a in axes]
    route = []
    for i in range(math.prod(dims)):
        rest, at = i, {}
        for a, n in reversed(list(zip(axes, dims))):
            at[a], rest = rest % n, rest // n
        to = move(dict(at))
        j = 0
        for a, n in zip(axes, dims):
            j = j * n + to[a] % n
        route.append((i, j))
    return route


def shifted(block, axis, k):
    return lax.ppermute(block, axis, pairs((axis,), lambda at: {axis: at[axis] + k}))


def crossed(block, first, second, k):
    def move(at):
        along = first if at["cfg"] == 0 else second
        at[along] += k
        return at

    axes = ("cfg", "y", "x")
    return lax.ppermute(block, axes, pairs(axes, move))


def code_of(largest):
    return jnp.ceil(jnp.log(jnp.maximum(largest, 1e-30)) * (1.0 / STEP)) + 1.0


def scale_of(code):
    return jnp.exp(code * STEP) * (1.0 / TOP)


def coded(values, scale):
    return jnp.clip(jnp.round(values / scale), -TOP, TOP).astype(jnp.int32).astype(jnp.int16)


def in_vmem(count):
    return [pl.BlockSpec(memory_space=pltpu.VMEM)] * count


def room(mib):
    return pltpu.CompilerParams(vmem_limit_bytes=mib << 20)


def load_kernel(head_ref, out_ref, done):
    copy = pltpu.make_async_copy(head_ref, out_ref, done)
    copy.start()
    copy.wait()


def load(head):
    return pl.pallas_call(
        load_kernel,
        out_shape=jax.ShapeDtypeStruct(head.shape, head.dtype),
        in_specs=[pl.BlockSpec(memory_space=pl.ANY)],
        out_specs=in_vmem(1)[0],
        scratch_shapes=[pltpu.SemaphoreType.DMA],
        compiler_params=room(44),
        cost_estimate=pl.CostEstimate(flops=0, bytes_accessed=16 << 20, transcendentals=0),
        name="load",
    )(head)


def mix_kernel(place_ref, own_ref, other_ref, own_scale_ref, away_scale_ref, out_ref):
    core, far = place_ref[0], place_ref[1]
    first = core == 0
    for n, half in enumerate((1 - far, far)):
        cut = pl.ds(pl.multiple_of(half * 512 + core * 256, 256), 256)
        scale_ref = away_scale_ref if n == 0 else own_scale_ref
        scales = scale_ref[:, pl.ds(pl.multiple_of(core * 256, 256), 256)]
        guide = 1.0 + 0.5 * scales.astype(jnp.float32)
        own = own_ref[:, cut].astype(jnp.float32)
        other = other_ref[:, cut].astype(jnp.float32)
        cond = jnp.where(first, own, other)
        uncond = jnp.where(first, other, own)
        mixed = uncond + guide * (cond - uncond)
        code = code_of(jnp.max(jnp.abs(mixed), axis=0, keepdims=True))
        at = slice(256 * n, 256 * n + 256)
        out_ref[:64, at] = coded(mixed, scale_of(code))
        out_ref[64:, at] = jnp.broadcast_to(code, (16, 256)).astype(jnp.int32).astype(jnp.int16)


def mix(place, own, other, own_scale, away_scale):
    return pl.pallas_call(
        mix_kernel,
        out_shape=jax.ShapeDtypeStruct((80, 512), jnp.int16),
        in_specs=[pl.BlockSpec(memory_space=pltpu.SMEM)] + in_vmem(4),
        out_specs=in_vmem(1)[0],
        compiler_params=room(4),
        name="mix",
    )(place, own, other, own_scale, away_scale)


def stack_kernel(place_ref, a_ref, b_ref, c_ref, d_ref, out_ref):
    width = a_ref.shape[1]
    row = lax.broadcasted_iota(jnp.int32, (16, width), 0)
    codes = jnp.zeros((16, width), jnp.int32)
    for k, ref in enumerate((a_ref, b_ref, c_ref, d_ref)):
        place = (place_ref[4] - k) & 3
        out_ref[pl.ds(pl.multiple_of(place * 64, 64), 64), :] = ref[:64]
        codes = jnp.where(row == place, ref[64:].astype(jnp.int32), codes)
    out_ref[256:] = codes.astype(jnp.int16)


def stack(place, parts):
    return pl.pallas_call(
        stack_kernel,
        out_shape=jax.ShapeDtypeStruct((272, parts[0].shape[1]), jnp.int16),
        in_specs=[pl.BlockSpec(memory_space=pltpu.SMEM)] + in_vmem(4),
        out_specs=in_vmem(1)[0],
        compiler_params=room(4),
        name="stack",
    )(place, *parts)


def pack_kernel(start, *refs):
    out_ref = refs[-1]
    for k in range(4):
        out_ref[272 * k : 272 * k + 272] = refs[k][:, start : start + out_ref.shape[1]]


def pack(line, start, count, after):
    return pl.pallas_call(
        functools.partial(pack_kernel, start),
        out_shape=jax.ShapeDtypeStruct((1088, count), jnp.int16),
        in_specs=in_vmem(4) + [pl.BlockSpec(memory_space=pl.ANY)] * len(after),
        out_specs=in_vmem(1)[0],
        compiler_params=room(4),
        name="pack",
    )(*line, *after)


def product_kernel(place_ref, head_ref, *refs):
    parts, out_ref, total_ref = refs[:4], refs[4], refs[5]
    core, y, x = place_ref[0], place_ref[2], place_ref[3]
    count = total_ref.shape[0] // 2
    dims = (((0,), (0,)), ((), ()))
    for k, part in enumerate(parts):
        total = None
        for piece in range(4):
            base = 272 * piece
            scale = scale_of(part[base + 256 : base + 272].astype(jnp.float32))
            high, low = [], []
            for j in range(4):
                values = part[base + 64 * j : base + 64 * j + 64].astype(jnp.float32) * scale[j : j + 1]
                top = values.astype(jnp.bfloat16)
                high.append(top)
                low.append((values - top.astype(jnp.float32)).astype(jnp.bfloat16))
            both = jnp.concatenate([jnp.concatenate(high, 0), jnp.concatenate(low, 0)], 1)
            row = jnp.where(core == 0, y - k, y - piece) & 3
            column = jnp.where(core == 0, x - piece, x - k) & 3
            weight = head_ref[pl.ds(pl.multiple_of((row * 4 + column) * 256, 256), 256), :]
            term = lax.dot_general(both, weight, dims, preferred_element_type=jnp.float32)
            total = term if total is None else total + term
        if k == 0:
            total_ref[...] = total
        else:
            total_ref[...] += total
    total = total_ref[:count] + total_ref[count:]
    if out_ref.dtype == jnp.float32:
        out_ref[...] = total
    else:
        code = code_of(jnp.max(jnp.abs(total), axis=1, keepdims=True))
        out_ref[:count] = coded(total, scale_of(code))
        across = jnp.transpose(jnp.broadcast_to(code, (count, 128)))[:16]
        out_ref[count:] = jnp.zeros((16, total.shape[1]), jnp.int16)
        out_ref[count:, :count] = across.astype(jnp.int32).astype(jnp.int16)


def product(place, head, parts, keep):
    tokens, width = parts[0].shape[1], head.shape[1]
    out = (
        jax.ShapeDtypeStruct((tokens, width), jnp.float32)
        if keep
        else jax.ShapeDtypeStruct((tokens + 16, width), jnp.int16)
    )
    return pl.pallas_call(
        product_kernel,
        out_shape=out,
        in_specs=[pl.BlockSpec(memory_space=pltpu.SMEM)] + in_vmem(5),
        out_specs=in_vmem(1)[0],
        scratch_shapes=[pltpu.VMEM((2 * tokens, width), jnp.float32)],
        compiler_params=room(24),
        cost_estimate=pl.CostEstimate(
            flops=4 * tokens * 4096 * width, bytes_accessed=10 << 20, transcendentals=0
        ),
        name="product",
    )(place, head, *parts)


def join_kernel(kept_ref, *refs):
    backs, guided_ref, stats_ref = refs[:-2], refs[-2], refs[-1]
    start = 0
    for back_ref in backs:
        count = back_ref.shape[0] - 16
        rows = slice(start, start + count)
        codes = back_ref[count:, :count].astype(jnp.float32)[:1]
        scale = jnp.transpose(jnp.broadcast_to(scale_of(codes), (128, count)))[:, :1]
        guided = kept_ref[rows] + back_ref[:count].astype(jnp.float32) * scale
        peak = jnp.max(guided, axis=1, keepdims=True)
        expo = jnp.exp(guided - peak)
        total = jnp.sum(expo, axis=1, keepdims=True)
        moment = jnp.sum(expo * guided, axis=1, keepdims=True)
        lane = lax.broadcasted_iota(jnp.int32, (count, 128), 1)
        table = jnp.where(lane == 0, peak + jnp.log(total), moment / total)
        own = jnp.transpose(table)
        for at in range(0, count, 128):
            for i in range(2):
                spot = 2 * i + (start + at) // 128
                line = own[i : i + 1, at : at + 128]
                stats_ref[:, spot : spot + 1] = jnp.broadcast_to(line[None], (64, 1, 128))
        guided_ref[rows] = guided
        start += count
    stats_ref[:, 4:] = jnp.zeros((64, 4, 128), jnp.float32)


def join(kept, backs):
    return pl.pallas_call(
        join_kernel,
        out_shape=(
            jax.ShapeDtypeStruct(kept.shape, jnp.float32),
            jax.ShapeDtypeStruct((64, 8, 128), jnp.float32),
        ),
        in_specs=in_vmem(1 + len(backs)),
        out_specs=in_vmem(2),
        compiler_params=room(12),
        name="join",
    )(kept, *backs)


def local(hidden, head, scale_index, threshold):
    core, far = lax.axis_index("cfg"), lax.axis_index("zh")
    y, x, zl = lax.axis_index("y"), lax.axis_index("x"), lax.axis_index("zl")
    slot = jnp.arange(8)
    place = jnp.zeros((8,), jnp.int32)
    for i, at in enumerate((core, far, y, x, zl)):
        place = jnp.where(slot == i, at, place)
    features = hidden[0].T
    other = lax.ppermute(features, "cfg", [(0, 1), (1, 0)])
    away_scale = lax.ppermute(scale_index, "zh", [(0, 1), (1, 0)])
    limits = lax.dynamic_slice_in_dim(threshold, core * 256, 256, 0).astype(jnp.float32) / 8.0

    mixed = mix(place, features, other, scale_index[None], away_scale[None])
    head = load(lax.optimization_barrier((head, mixed))[0])
    near = [mixed] + [shifted(mixed, "zl", k) for k in (1, 2, 3)]
    column = stack(place, near)

    def spread(block, first, second):
        return [block] + [crossed(block, first, second, k) for k in (1, 2, 3)]

    line = spread(column, "x", "y")
    backs, before = [], (head,)
    for start, count in CHUNKS:
        if start == 128:
            before = before[1:2]
        before = spread(pack(line, start, count, before), "y", "x")
        result = product(place, head, before, start >= 256)
        if start < 256:
            backs.append(lax.ppermute(result, "zh", [(0, 1), (1, 0)]))

    guided, stats = join(result, backs)
    stats = lax.all_to_all(stats, ("y", "x", "zl"), 0, 0, tiled=True)
    each, mean = stats[:, :2], stats[:, 2:4]
    top = jnp.max(each, axis=0)
    weight = jnp.exp(each - top)
    total = jnp.sum(weight, axis=0)
    lse = top + jnp.log(total)
    entropy = lse - jnp.sum(weight * mean, axis=0) / total
    lse, entropy = lse.reshape(256), entropy.reshape(256)
    logprob = guided - lse[:, None]
    deviation = -logprob - entropy[:, None]
    typical = jax.nn.sigmoid(2.0 * (limits[:, None] - jnp.abs(deviation)))
    return logprob.astype(jnp.bfloat16), typical.astype(jnp.bfloat16), entropy


def solution(mesh):
    torus = Mesh(mesh.devices.reshape(SIZES), AXES)
    vocab = ("y", "x", "zl")
    return jax.shard_map(
        local,
        mesh=torus,
        in_specs=(P("cfg", None, ("zh", *vocab)), P("zh", vocab), P("zh"), P("zh")),
        out_specs=(P(("zh", "cfg"), vocab), P(("zh", "cfg"), vocab), P(("zh", "cfg"))),
        check_vma=False,
    )
```

```python
import math

import jax
import jax.numpy as jnp
from jax import lax
from jax.experimental import pallas as pl
from jax.experimental.pallas import tpu as pltpu
from jax.sharding import Mesh, PartitionSpec as P

AXES = ("cfg", "y", "x", "zl", "zh")
SIZES = (2, 4, 4, 4, 2)
TOP = 32767.0
STEP = math.log(2.0) / 256.0


def pairs(axes, move):
    dims = [SIZES[AXES.index(a)] for a in axes]
    route = []
    for i in range(math.prod(dims)):
        rest, at = i, {}
        for a, n in reversed(list(zip(axes, dims))):
            at[a], rest = rest % n, rest // n
        to = move(dict(at))
        j = 0
        for a, n in zip(axes, dims):
            j = j * n + to[a] % n
        route.append((i, j))
    return route


def shifted(block, axis, k):
    return lax.ppermute(block, axis, pairs((axis,), lambda at: {axis: at[axis] + k}))


def crossed(block, first, second, k):
    def move(at):
        along = first if at["cfg"] == 0 else second
        at[along] += k
        return at

    axes = ("cfg", "y", "x")
    return lax.ppermute(block, axes, pairs(axes, move))


def code_of(largest):
    return jnp.ceil(jnp.log(jnp.maximum(largest, 1e-30)) * (1.0 / STEP)) + 1.0


def scale_of(code):
    return jnp.exp(code * STEP) * (1.0 / TOP)


def coded(values, scale):
    return jnp.clip(jnp.round(values / scale), -TOP, TOP).astype(jnp.int32).astype(jnp.int16)


def in_vmem(count):
    return [pl.BlockSpec(memory_space=pltpu.VMEM)] * count


def anywhere(arrays):
    return [pl.BlockSpec(memory_space=pl.ANY)] * len(arrays)


def room(mib):
    return pltpu.CompilerParams(vmem_limit_bytes=mib << 20)


def load_kernel(*refs):
    count = len(refs) // 2
    copies = [pltpu.make_async_copy(refs[i], refs[count + i], refs[-1].at[i]) for i in range(count)]
    for copy in copies:
        copy.start()
    for copy in copies:
        copy.wait()


def load(*arrays):
    return pl.pallas_call(
        load_kernel,
        out_shape=[jax.ShapeDtypeStruct(a.shape, a.dtype) for a in arrays],
        in_specs=anywhere(arrays),
        out_specs=in_vmem(len(arrays)),
        scratch_shapes=[pltpu.SemaphoreType.DMA((len(arrays),))],
        compiler_params=room(44),
        cost_estimate=pl.CostEstimate(
            flops=0, bytes_accessed=2 * sum(a.size * a.dtype.itemsize for a in arrays), transcendentals=0
        ),
        name="load",
    )(*arrays)


def mix_kernel(place_ref, own_ref, other_ref, own_scale_ref, away_scale_ref, *out_refs):
    core, far = place_ref[0], place_ref[1]
    first = core == 0
    for n, half in enumerate((1 - far, far)):
        cut = pl.ds(pl.multiple_of(half * 512 + core * 256, 256), 256)
        scale_ref = away_scale_ref if n == 0 else own_scale_ref
        scales = scale_ref[:, pl.ds(pl.multiple_of(core * 256, 256), 256)]
        guide = 1.0 + 0.5 * scales.astype(jnp.float32)
        own = own_ref[:, cut].astype(jnp.float32)
        other = other_ref[:, cut].astype(jnp.float32)
        cond = jnp.where(first, own, other)
        uncond = jnp.where(first, other, own)
        mixed = uncond + guide * (cond - uncond)
        code = code_of(jnp.max(jnp.abs(mixed), axis=0, keepdims=True))
        out_refs[n][:64] = coded(mixed, scale_of(code))
        out_refs[n][64:] = jnp.broadcast_to(code, (16, 256)).astype(jnp.int32).astype(jnp.int16)


def mix(place, own, other, own_scale, away_scale):
    return pl.pallas_call(
        mix_kernel,
        out_shape=[jax.ShapeDtypeStruct((80, 256), jnp.int16)] * 2,
        in_specs=[pl.BlockSpec(memory_space=pltpu.SMEM)] + in_vmem(4),
        out_specs=in_vmem(2),
        compiler_params=room(4),
        name="mix",
    )(place, own, other, own_scale, away_scale)


def hold_kernel(block_ref, *refs):
    refs[-1][...] = block_ref[...]


def hold(block, after):
    return pl.pallas_call(
        hold_kernel,
        out_shape=jax.ShapeDtypeStruct(block.shape, block.dtype),
        in_specs=in_vmem(1) + anywhere(after),
        out_specs=in_vmem(1)[0],
        compiler_params=room(4),
        name="hold",
    )(block, *after)


def stack_kernel(place_ref, a_ref, b_ref, c_ref, d_ref, *refs):
    out_ref = refs[-1]
    width = a_ref.shape[1]
    row = lax.broadcasted_iota(jnp.int32, (16, width), 0)
    codes = jnp.zeros((16, width), jnp.int32)
    for k, ref in enumerate((a_ref, b_ref, c_ref, d_ref)):
        place = (place_ref[4] - k) & 3
        out_ref[pl.ds(pl.multiple_of(place * 64, 64), 64), :] = ref[:64]
        codes = jnp.where(row == place, ref[64:].astype(jnp.int32), codes)
    out_ref[256:] = codes.astype(jnp.int16)


def stack(place, parts, after):
    return pl.pallas_call(
        stack_kernel,
        out_shape=jax.ShapeDtypeStruct((272, parts[0].shape[1]), jnp.int16),
        in_specs=[pl.BlockSpec(memory_space=pltpu.SMEM)] + in_vmem(4) + anywhere(after),
        out_specs=in_vmem(1)[0],
        compiler_params=room(4),
        name="stack",
    )(place, *parts, *after)


def pack_kernel(*refs):
    for k in range(4):
        refs[-1][272 * k : 272 * k + 272] = refs[k][...]


def pack(line, after):
    return pl.pallas_call(
        pack_kernel,
        out_shape=jax.ShapeDtypeStruct((1088, line[0].shape[1]), jnp.int16),
        in_specs=in_vmem(4) + anywhere(after),
        out_specs=in_vmem(1)[0],
        compiler_params=room(4),
        name="pack",
    )(*line, *after)


def product_kernel(place_ref, head_ref, *refs):
    parts, out_ref, total_ref = refs[:4], refs[-2], refs[-1]
    core, y, x = place_ref[0], place_ref[2], place_ref[3]
    count = total_ref.shape[0] // 2
    dims = (((0,), (0,)), ((), ()))
    for k, part in enumerate(parts):
        total = None
        for piece in range(4):
            base = 272 * piece
            scale = scale_of(part[base + 256 : base + 272].astype(jnp.float32))
            high, low = [], []
            for j in range(4):
                values = part[base + 64 * j : base + 64 * j + 64].astype(jnp.float32) * scale[j : j + 1]
                top = values.astype(jnp.bfloat16)
                high.append(top)
                low.append((values - top.astype(jnp.float32)).astype(jnp.bfloat16))
            both = jnp.concatenate([jnp.concatenate(high, 0), jnp.concatenate(low, 0)], 1)
            row = jnp.where(core == 0, y - k, y - piece) & 3
            column = jnp.where(core == 0, x - piece, x - k) & 3
            weight = head_ref[pl.ds(pl.multiple_of((row * 4 + column) * 256, 256), 256), :]
            term = lax.dot_general(both, weight, dims, preferred_element_type=jnp.float32)
            total = term if total is None else total + term
        if k == 0:
            total_ref[...] = total
        else:
            total_ref[...] += total
    total = total_ref[:count] + total_ref[count:]
    if out_ref.dtype == jnp.float32:
        out_ref[...] = total
    else:
        code = code_of(jnp.max(jnp.abs(total), axis=1, keepdims=True))
        out_ref[:count] = coded(total, scale_of(code))
        across = jnp.transpose(jnp.broadcast_to(code, (count, 128)))[:16]
        out_ref[count:] = jnp.zeros((16, total.shape[1]), jnp.int16)
        out_ref[count:, :count] = across.astype(jnp.int32).astype(jnp.int16)


def product(place, head, parts, keep, after):
    tokens, width = parts[0].shape[1], head.shape[1]
    out = (
        jax.ShapeDtypeStruct((tokens, width), jnp.float32)
        if keep
        else jax.ShapeDtypeStruct((tokens + 16, width), jnp.int16)
    )
    return pl.pallas_call(
        product_kernel,
        out_shape=out,
        in_specs=[pl.BlockSpec(memory_space=pltpu.SMEM)] + in_vmem(5) + anywhere(after),
        out_specs=in_vmem(1)[0],
        scratch_shapes=[pltpu.VMEM((2 * tokens, width), jnp.float32)],
        compiler_params=room(24),
        cost_estimate=pl.CostEstimate(
            flops=4 * tokens * 4096 * width, bytes_accessed=10 << 20, transcendentals=0
        ),
        name="product",
    )(place, head, *parts, *after)


def join_kernel(kept_ref, back_ref, guided_ref, stats_ref):
    codes = back_ref[256:, :256].astype(jnp.float32)[:1]
    scale = jnp.transpose(jnp.broadcast_to(scale_of(codes), (128, 256)))[:, :1]
    guided = kept_ref[...] + back_ref[:256].astype(jnp.float32) * scale
    peak = jnp.max(guided, axis=1, keepdims=True)
    expo = jnp.exp(guided - peak)
    total = jnp.sum(expo, axis=1, keepdims=True)
    moment = jnp.sum(expo * guided, axis=1, keepdims=True)
    lane = lax.broadcasted_iota(jnp.int32, (256, 128), 1)
    table = jnp.transpose(jnp.where(lane == 0, peak + jnp.log(total), moment / total))
    rows = [table[i : i + 1, at : at + 128] for i in (0, 1) for at in (0, 128)]
    tile = jnp.concatenate(rows + [jnp.zeros((4, 128), jnp.float32)], 0)
    stats_ref[...] = jnp.broadcast_to(tile[None], (64, 8, 128))
    guided_ref[...] = guided


def join(kept, back):
    return pl.pallas_call(
        join_kernel,
        out_shape=(
            jax.ShapeDtypeStruct(kept.shape, jnp.float32),
            jax.ShapeDtypeStruct((64, 8, 128), jnp.float32),
        ),
        in_specs=in_vmem(2),
        out_specs=in_vmem(2),
        compiler_params=room(12),
        name="join",
    )(kept, back)


def local(hidden, head, scale_index, threshold):
    core, far = lax.axis_index("cfg"), lax.axis_index("zh")
    y, x, zl = lax.axis_index("y"), lax.axis_index("x"), lax.axis_index("zl")
    slot = jnp.arange(8)
    place = jnp.zeros((8,), jnp.int32)
    for i, at in enumerate((core, far, y, x, zl)):
        place = jnp.where(slot == i, at, place)
    features = hidden[0].T
    other = lax.ppermute(features, "cfg", [(0, 1), (1, 0)])
    away_scale = lax.ppermute(scale_index, "zh", [(0, 1), (1, 0)])
    limits = lax.dynamic_slice_in_dim(threshold, core * 256, 256, 0).astype(jnp.float32) / 8.0

    own, own_scale = load(features, scale_index[None])
    away, home = mix(place, own, other, own_scale, away_scale[None])
    (head,) = load(lax.optimization_barrier((head, away))[0])

    def near(block):
        return [block] + [shifted(block, "zl", k) for k in (1, 2, 3)]

    def spread(block, first, second):
        return [block] + [crossed(block, first, second, k) for k in (1, 2, 3)]

    away_near = near(away)
    home_near = near(hold(home, away_near[1:]))
    away_line = spread(stack(place, away_near, (head,)), "x", "y")
    away_block = pack(away_line, ())
    away_parts = spread(away_block, "y", "x")
    home_line = spread(stack(place, home_near, (away_block,)), "x", "y")
    sent = product(place, head, away_parts, False, ())
    back = lax.ppermute(sent, "zh", [(0, 1), (1, 0)])
    home_parts = spread(pack(home_line, (sent,)), "y", "x")
    kept = product(place, head, home_parts, True, ())

    guided, stats = join(kept, back)
    stats = lax.all_to_all(stats, ("y", "x", "zl"), 0, 0, tiled=True)
    each, mean = stats[:, :2], stats[:, 2:4]
    top = jnp.max(each, axis=0)
    weight = jnp.exp(each - top)
    total = jnp.sum(weight, axis=0)
    lse = top + jnp.log(total)
    entropy = lse - jnp.sum(weight * mean, axis=0) / total
    lse, entropy = lse.reshape(256), entropy.reshape(256)
    logprob = guided - lse[:, None]
    deviation = -logprob - entropy[:, None]
    typical = jax.nn.sigmoid(2.0 * (limits[:, None] - jnp.abs(deviation)))
    return logprob.astype(jnp.bfloat16), typical.astype(jnp.bfloat16), entropy


def solution(mesh):
    torus = Mesh(mesh.devices.reshape(SIZES), AXES)
    vocab = ("y", "x", "zl")
    return jax.shard_map(
        local,
        mesh=torus,
        in_specs=(P("cfg", None, ("zh", *vocab)), P("zh", vocab), P("zh"), P("zh")),
        out_specs=(P(("zh", "cfg"), vocab), P(("zh", "cfg"), vocab), P(("zh", "cfg"))),
        check_vma=False,
    )
```

```python
import math

import jax
import jax.numpy as jnp
from jax import lax
from jax.experimental import pallas as pl
from jax.experimental.pallas import tpu as pltpu
from jax.sharding import Mesh, PartitionSpec as P

AXES = ("cfg", "y", "x", "zl", "zh")
SIZES = (2, 4, 4, 4, 2)
TOP = 32767.0
STEP = math.log(2.0) / 256.0


def pairs(axes, move):
    dims = [SIZES[AXES.index(a)] for a in axes]
    route = []
    for i in range(math.prod(dims)):
        rest, at = i, {}
        for a, n in reversed(list(zip(axes, dims))):
            at[a], rest = rest % n, rest // n
        to = move(dict(at))
        j = 0
        for a, n in zip(axes, dims):
            j = j * n + to[a] % n
        route.append((i, j))
    return route


def shifted(block, axis, k):
    return lax.ppermute(block, axis, pairs((axis,), lambda at: {axis: at[axis] + k}))


def crossed(block, first, second, k):
    def move(at):
        along = first if at["cfg"] == 0 else second
        at[along] += k
        return at

    axes = ("cfg", "y", "x")
    return lax.ppermute(block, axes, pairs(axes, move))


def nearest_other(at):
    z = at["zh"] * 4 + at["zl"]
    z = (z + (2 if z % 4 >= 2 else 6)) % 8
    return {"zh": z // 4, "zl": z % 4}


def code_of(largest):
    return jnp.ceil(jnp.log(jnp.maximum(largest, 1e-30)) * (1.0 / STEP)) + 1.0


def scale_of(code):
    return jnp.exp(code * STEP) * (1.0 / TOP)


def coded(values, scale):
    return jnp.clip(jnp.round(values / scale), -TOP, TOP).astype(jnp.int32).astype(jnp.int16)


def in_vmem(count):
    return [pl.BlockSpec(memory_space=pltpu.VMEM)] * count


def anywhere(arrays):
    return [pl.BlockSpec(memory_space=pl.ANY)] * len(arrays)


def room(mib):
    return pltpu.CompilerParams(vmem_limit_bytes=mib << 20)


def load_kernel(*refs):
    count = len(refs) // 2
    copies = [pltpu.make_async_copy(refs[i], refs[count + i], refs[-1].at[i]) for i in range(count)]
    for copy in copies:
        copy.start()
    for copy in copies:
        copy.wait()


def load(*arrays):
    return pl.pallas_call(
        load_kernel,
        out_shape=[jax.ShapeDtypeStruct(a.shape, a.dtype) for a in arrays],
        in_specs=anywhere(arrays),
        out_specs=in_vmem(len(arrays)),
        scratch_shapes=[pltpu.SemaphoreType.DMA((len(arrays),))],
        compiler_params=room(44),
        cost_estimate=pl.CostEstimate(
            flops=0, bytes_accessed=2 * sum(a.size * a.dtype.itemsize for a in arrays), transcendentals=0
        ),
        name="load",
    )(*arrays)


def mix_kernel(place_ref, own_ref, other_ref, own_scale_ref, away_scale_ref, *out_refs):
    core, far = place_ref[0], place_ref[1]
    first = core == 0
    for n, half in enumerate((1 - far, far)):
        cut = pl.ds(pl.multiple_of(half * 512 + core * 256, 256), 256)
        scale_ref = away_scale_ref if n == 0 else own_scale_ref
        scales = scale_ref[:, pl.ds(pl.multiple_of(core * 256, 256), 256)]
        guide = 1.0 + 0.5 * scales.astype(jnp.float32)
        own = own_ref[:, cut].astype(jnp.float32)
        other = other_ref[:, cut].astype(jnp.float32)
        cond = jnp.where(first, own, other)
        uncond = jnp.where(first, other, own)
        mixed = uncond + guide * (cond - uncond)
        code = code_of(jnp.max(jnp.abs(mixed), axis=0, keepdims=True))
        out_refs[n][:64] = coded(mixed, scale_of(code))
        out_refs[n][64:] = jnp.broadcast_to(code, (16, 256)).astype(jnp.int32).astype(jnp.int16)


def mix(place, own, other, own_scale, away_scale):
    return pl.pallas_call(
        mix_kernel,
        out_shape=[jax.ShapeDtypeStruct((80, 256), jnp.int16)] * 2,
        in_specs=[pl.BlockSpec(memory_space=pltpu.SMEM)] + in_vmem(4),
        out_specs=in_vmem(2),
        compiler_params=room(4),
        name="mix",
    )(place, own, other, own_scale, away_scale)


def stack_kernel(place_ref, a_ref, b_ref, c_ref, d_ref, *refs):
    out_ref = refs[-1]
    width = a_ref.shape[1]
    row = lax.broadcasted_iota(jnp.int32, (16, width), 0)
    codes = jnp.zeros((16, width), jnp.int32)
    for k, ref in enumerate((a_ref, b_ref, c_ref, d_ref)):
        place = (place_ref[4] - k) & 3
        out_ref[pl.ds(pl.multiple_of(place * 64, 64), 64), :] = ref[:64]
        codes = jnp.where(row == place, ref[64:].astype(jnp.int32), codes)
    out_ref[256:] = codes.astype(jnp.int16)


def stack(place, parts, after):
    return pl.pallas_call(
        stack_kernel,
        out_shape=jax.ShapeDtypeStruct((272, parts[0].shape[1]), jnp.int16),
        in_specs=[pl.BlockSpec(memory_space=pltpu.SMEM)] + in_vmem(4) + anywhere(after),
        out_specs=in_vmem(1)[0],
        compiler_params=room(4),
        name="stack",
    )(place, *parts, *after)


def pack_kernel(*refs):
    for k in range(4):
        refs[-1][272 * k : 272 * k + 272] = refs[k][...]


def pack(line, after):
    return pl.pallas_call(
        pack_kernel,
        out_shape=jax.ShapeDtypeStruct((1088, line[0].shape[1]), jnp.int16),
        in_specs=in_vmem(4) + anywhere(after),
        out_specs=in_vmem(1)[0],
        compiler_params=room(4),
        name="pack",
    )(*line, *after)


def product_kernel(place_ref, head_ref, *refs):
    parts, out_ref, total_ref = refs[:4], refs[-2], refs[-1]
    core, y, x = place_ref[0], place_ref[2], place_ref[3]
    count = total_ref.shape[0] // 2
    dims = (((0,), (0,)), ((), ()))
    for k, part in enumerate(parts):
        total = None
        for piece in range(4):
            base = 272 * piece
            scale = scale_of(part[base + 256 : base + 272].astype(jnp.float32))
            high, low = [], []
            for j in range(4):
                values = part[base + 64 * j : base + 64 * j + 64].astype(jnp.float32) * scale[j : j + 1]
                top = values.astype(jnp.bfloat16)
                high.append(top)
                low.append((values - top.astype(jnp.float32)).astype(jnp.bfloat16))
            both = jnp.concatenate([jnp.concatenate(high, 0), jnp.concatenate(low, 0)], 1)
            row = jnp.where(core == 0, y - k, y - piece) & 3
            column = jnp.where(core == 0, x - piece, x - k) & 3
            weight = head_ref[pl.ds(pl.multiple_of((row * 4 + column) * 256, 256), 256), :]
            term = lax.dot_general(both, weight, dims, preferred_element_type=jnp.float32)
            total = term if total is None else total + term
        if k == 0:
            total_ref[...] = total
        else:
            total_ref[...] += total
    total = total_ref[:count] + total_ref[count:]
    if out_ref.dtype == jnp.float32:
        out_ref[...] = total
    else:
        code = code_of(jnp.max(jnp.abs(total), axis=1, keepdims=True))
        out_ref[:count] = coded(total, scale_of(code))
        across = jnp.transpose(jnp.broadcast_to(code, (count, 128)))[:16]
        out_ref[count:] = jnp.zeros((16, total.shape[1]), jnp.int16)
        out_ref[count:, :count] = across.astype(jnp.int32).astype(jnp.int16)


def product(place, head, parts, keep, after):
    tokens, width = parts[0].shape[1], head.shape[1]
    out = (
        jax.ShapeDtypeStruct((tokens, width), jnp.float32)
        if keep
        else jax.ShapeDtypeStruct((tokens + 16, width), jnp.int16)
    )
    return pl.pallas_call(
        product_kernel,
        out_shape=out,
        in_specs=[pl.BlockSpec(memory_space=pltpu.SMEM)] + in_vmem(5) + anywhere(after),
        out_specs=in_vmem(1)[0],
        scratch_shapes=[pltpu.VMEM((2 * tokens, width), jnp.float32)],
        compiler_params=room(24),
        cost_estimate=pl.CostEstimate(
            flops=4 * tokens * 4096 * width, bytes_accessed=10 << 20, transcendentals=0
        ),
        name="product",
    )(place, head, *parts, *after)


def join_kernel(kept_ref, back_ref, guided_ref, stats_ref):
    codes = back_ref[256:, :256].astype(jnp.float32)[:1]
    scale = jnp.transpose(jnp.broadcast_to(scale_of(codes), (128, 256)))[:, :1]
    guided = kept_ref[...] + back_ref[:256].astype(jnp.float32) * scale
    peak = jnp.max(guided, axis=1, keepdims=True)
    expo = jnp.exp(guided - peak)
    total = jnp.sum(expo, axis=1, keepdims=True)
    moment = jnp.sum(expo * guided, axis=1, keepdims=True)
    lane = lax.broadcasted_iota(jnp.int32, (256, 128), 1)
    table = jnp.transpose(jnp.where(lane == 0, peak + jnp.log(total), moment / total))
    rows = [table[i : i + 1, at : at + 128] for i in (0, 1) for at in (0, 128)]
    tile = jnp.concatenate(rows + [jnp.zeros((4, 128), jnp.float32)], 0)
    stats_ref[...] = jnp.broadcast_to(tile[None], (64, 8, 128))
    guided_ref[...] = guided


def join(kept, back):
    return pl.pallas_call(
        join_kernel,
        out_shape=(
            jax.ShapeDtypeStruct(kept.shape, jnp.float32),
            jax.ShapeDtypeStruct((64, 8, 128), jnp.float32),
        ),
        in_specs=in_vmem(2),
        out_specs=in_vmem(2),
        compiler_params=room(12),
        name="join",
    )(kept, back)


def local(hidden, head, scale_index, threshold):
    core, far = lax.axis_index("cfg"), lax.axis_index("zh")
    y, x, zl = lax.axis_index("y"), lax.axis_index("x"), lax.axis_index("zl")
    slot = jnp.arange(8)
    place = jnp.zeros((8,), jnp.int32)
    for i, at in enumerate((core, far, y, x, zl)):
        place = jnp.where(slot == i, at, place)
    features = hidden[0].T
    other = lax.ppermute(features, "cfg", [(0, 1), (1, 0)])
    away_scale = lax.ppermute(scale_index, ("zl", "zh"), pairs(("zl", "zh"), nearest_other))
    limits = lax.dynamic_slice_in_dim(threshold, core * 256, 256, 0).astype(jnp.float32) / 8.0

    own, own_scale = load(features, scale_index[None])
    away, home = mix(place, own, other, own_scale, away_scale[None])
    (head,) = load(lax.optimization_barrier((head, away))[0])

    def near(block):
        return [block] + [shifted(block, "zl", k) for k in (1, 2, 3)]

    def spread(block, first, second):
        return [block] + [crossed(block, first, second, k) for k in (1, 2, 3)]

    away_near = near(away)
    home_near = near(home)
    away_column = stack(place, away_near, (head,))
    away_line = spread(away_column, "x", "y")
    home_column = stack(place, home_near, (away_column,))
    home_line = spread(home_column, "x", "y")
    away_parts = spread(pack(away_line, (home_column,)), "y", "x")
    sent = product(place, head, away_parts, False, ())
    back = lax.ppermute(sent, "zh", [(0, 1), (1, 0)])
    home_parts = spread(pack(home_line, (sent,)), "y", "x")
    kept = product(place, head, home_parts, True, ())

    guided, stats = join(kept, back)
    stats = lax.all_to_all(stats, ("y", "x", "zl"), 0, 0, tiled=True)
    each, mean = stats[:, :2], stats[:, 2:4]
    top = jnp.max(each, axis=0)
    weight = jnp.exp(each - top)
    total = jnp.sum(weight, axis=0)
    lse = top + jnp.log(total)
    entropy = lse - jnp.sum(weight * mean, axis=0) / total
    lse, entropy = lse.reshape(256), entropy.reshape(256)
    logprob = guided - lse[:, None]
    deviation = -logprob - entropy[:, None]
    typical = jax.nn.sigmoid(2.0 * (limits[:, None] - jnp.abs(deviation)))
    return logprob.astype(jnp.bfloat16), typical.astype(jnp.bfloat16), entropy


def solution(mesh):
    torus = Mesh(mesh.devices.reshape(SIZES), AXES)
    vocab = ("y", "x", "zl")
    return jax.shard_map(
        local,
        mesh=torus,
        in_specs=(P("cfg", None, ("zh", *vocab)), P("zh", vocab), P("zh"), P("zh")),
        out_specs=(P(("zh", "cfg"), vocab), P(("zh", "cfg"), vocab), P(("zh", "cfg"))),
        check_vma=False,
    )
```

```python
import math

import jax
import jax.numpy as jnp
from jax import lax
from jax.experimental import pallas as pl
from jax.experimental.pallas import tpu as pltpu
from jax.sharding import Mesh, PartitionSpec as P

AXES = ("cfg", "y", "x", "zl", "zh")
SIZES = (2, 4, 4, 4, 2)
TOP = 32767.0
STEP = math.log(2.0) / 256.0


def pairs(axes, move):
    dims = [SIZES[AXES.index(a)] for a in axes]
    route = []
    for i in range(math.prod(dims)):
        rest, at = i, {}
        for a, n in reversed(list(zip(axes, dims))):
            at[a], rest = rest % n, rest // n
        to = move(dict(at))
        j = 0
        for a, n in zip(axes, dims):
            j = j * n + to[a] % n
        route.append((i, j))
    return route


def shifted(block, axis, k):
    return lax.ppermute(block, axis, pairs((axis,), lambda at: {axis: at[axis] + k}))


def crossed(block, first, second, k):
    def move(at):
        along = first if at["cfg"] == 0 else second
        at[along] += k
        return at

    axes = ("cfg", "y", "x")
    return lax.ppermute(block, axes, pairs(axes, move))


def nearest_other(at):
    z = at["zh"] * 4 + at["zl"]
    z = (z + (2 if z % 4 >= 2 else 6)) % 8
    return {"zh": z // 4, "zl": z % 4}


def code_of(largest):
    return jnp.ceil(jnp.log(jnp.maximum(largest, 1e-30)) * (1.0 / STEP)) + 1.0


def scale_of(code):
    return jnp.exp(code * STEP) * (1.0 / TOP)


def coded(values, scale):
    return jnp.clip(jnp.round(values / scale), -TOP, TOP).astype(jnp.int32).astype(jnp.int16)


def in_vmem(count):
    return [pl.BlockSpec(memory_space=pltpu.VMEM)] * count


def anywhere(arrays):
    return [pl.BlockSpec(memory_space=pl.ANY)] * len(arrays)


def room(mib):
    return pltpu.CompilerParams(vmem_limit_bytes=mib << 20)


def load_kernel(*refs):
    count = len(refs) // 2
    copies = [pltpu.make_async_copy(refs[i], refs[count + i], refs[-1].at[i]) for i in range(count)]
    for copy in copies:
        copy.start()
    for copy in copies:
        copy.wait()


def load(*arrays):
    return pl.pallas_call(
        load_kernel,
        out_shape=[jax.ShapeDtypeStruct(a.shape, a.dtype) for a in arrays],
        in_specs=anywhere(arrays),
        out_specs=in_vmem(len(arrays)),
        scratch_shapes=[pltpu.SemaphoreType.DMA((len(arrays),))],
        compiler_params=room(44),
        cost_estimate=pl.CostEstimate(
            flops=0, bytes_accessed=2 * sum(a.size * a.dtype.itemsize for a in arrays), transcendentals=0
        ),
        name="load",
    )(*arrays)


def mix_kernel(place_ref, own_ref, other_ref, own_scale_ref, away_scale_ref, *out_refs):
    core, far = place_ref[0], place_ref[1]
    first = core == 0
    for n, half in enumerate((1 - far, far)):
        cut = pl.ds(pl.multiple_of(half * 512 + core * 256, 256), 256)
        scale_ref = away_scale_ref if n == 0 else own_scale_ref
        scales = scale_ref[:, pl.ds(pl.multiple_of(core * 256, 256), 256)]
        guide = 1.0 + 0.5 * scales.astype(jnp.float32)
        own = own_ref[:, cut].astype(jnp.float32)
        other = other_ref[:, cut].astype(jnp.float32)
        cond = jnp.where(first, own, other)
        uncond = jnp.where(first, other, own)
        mixed = uncond + guide * (cond - uncond)
        code = code_of(jnp.max(jnp.abs(mixed), axis=0, keepdims=True))
        out_refs[n][:64] = coded(mixed, scale_of(code))
        out_refs[n][64:] = jnp.broadcast_to(code, (16, 256)).astype(jnp.int32).astype(jnp.int16)


def mix(place, own, other, own_scale, away_scale):
    return pl.pallas_call(
        mix_kernel,
        out_shape=[jax.ShapeDtypeStruct((80, 256), jnp.int16)] * 2,
        in_specs=[pl.BlockSpec(memory_space=pltpu.SMEM)] + in_vmem(4),
        out_specs=in_vmem(2),
        compiler_params=room(4),
        name="mix",
    )(place, own, other, own_scale, away_scale)


def stack_kernel(place_ref, a_ref, b_ref, c_ref, d_ref, *refs):
    out_ref = refs[-1]
    width = a_ref.shape[1]
    row = lax.broadcasted_iota(jnp.int32, (16, width), 0)
    codes = jnp.zeros((16, width), jnp.int32)
    for k, ref in enumerate((a_ref, b_ref, c_ref, d_ref)):
        place = (place_ref[4] - k) & 3
        out_ref[pl.ds(pl.multiple_of(place * 64, 64), 64), :] = ref[:64]
        codes = jnp.where(row == place, ref[64:].astype(jnp.int32), codes)
    out_ref[256:] = codes.astype(jnp.int16)


def stack(place, parts, after):
    return pl.pallas_call(
        stack_kernel,
        out_shape=jax.ShapeDtypeStruct((272, parts[0].shape[1]), jnp.int16),
        in_specs=[pl.BlockSpec(memory_space=pltpu.SMEM)] + in_vmem(4) + anywhere(after),
        out_specs=in_vmem(1)[0],
        compiler_params=room(4),
        name="stack",
    )(place, *parts, *after)


def pack_kernel(*refs):
    for k in range(4):
        refs[-1][272 * k : 272 * k + 272] = refs[k][...]


def pack(line, after):
    return pl.pallas_call(
        pack_kernel,
        out_shape=jax.ShapeDtypeStruct((1088, line[0].shape[1]), jnp.int16),
        in_specs=in_vmem(4) + anywhere(after),
        out_specs=in_vmem(1)[0],
        compiler_params=room(4),
        name="pack",
    )(*line, *after)


def product_kernel(place_ref, head_ref, *refs):
    parts, out_ref, total_ref = refs[:4], refs[-2], refs[-1]
    core, y, x = place_ref[0], place_ref[2], place_ref[3]
    count = total_ref.shape[0] // 2
    dims = (((0,), (0,)), ((), ()))
    for k, part in enumerate(parts):
        total = None
        for piece in range(4):
            base = 272 * piece
            scale = scale_of(part[base + 256 : base + 272].astype(jnp.float32))
            high, low = [], []
            for j in range(4):
                values = part[base + 64 * j : base + 64 * j + 64].astype(jnp.float32) * scale[j : j + 1]
                top = values.astype(jnp.bfloat16)
                high.append(top)
                low.append((values - top.astype(jnp.float32)).astype(jnp.bfloat16))
            both = jnp.concatenate([jnp.concatenate(high, 0), jnp.concatenate(low, 0)], 1)
            row = jnp.where(core == 0, y - k, y - piece) & 3
            column = jnp.where(core == 0, x - piece, x - k) & 3
            weight = head_ref[pl.ds(pl.multiple_of((row * 4 + column) * 256, 256), 256), :]
            term = lax.dot_general(both, weight, dims, preferred_element_type=jnp.float32)
            total = term if total is None else total + term
        if k == 0:
            total_ref[...] = total
        else:
            total_ref[...] += total
    total = total_ref[:count] + total_ref[count:]
    if out_ref.dtype == jnp.float32:
        out_ref[...] = total
    else:
        code = code_of(jnp.max(jnp.abs(total), axis=1, keepdims=True))
        out_ref[:count] = coded(total, scale_of(code))
        across = jnp.transpose(jnp.broadcast_to(code, (count, 128)))[:16]
        out_ref[count:] = jnp.zeros((16, total.shape[1]), jnp.int16)
        out_ref[count:, :count] = across.astype(jnp.int32).astype(jnp.int16)


def product(place, head, parts, keep, after):
    tokens, width = parts[0].shape[1], head.shape[1]
    out = (
        jax.ShapeDtypeStruct((tokens, width), jnp.float32)
        if keep
        else jax.ShapeDtypeStruct((tokens + 16, width), jnp.int16)
    )
    return pl.pallas_call(
        product_kernel,
        out_shape=out,
        in_specs=[pl.BlockSpec(memory_space=pltpu.SMEM)] + in_vmem(5) + anywhere(after),
        out_specs=in_vmem(1)[0],
        scratch_shapes=[pltpu.VMEM((2 * tokens, width), jnp.float32)],
        compiler_params=room(24),
        cost_estimate=pl.CostEstimate(
            flops=4 * tokens * 4096 * width, bytes_accessed=10 << 20, transcendentals=0
        ),
        name="product",
    )(place, head, *parts, *after)


def join_kernel(kept_ref, back_ref, guided_ref, stats_ref):
    codes = back_ref[256:, :256].astype(jnp.float32)[:1]
    scale = jnp.transpose(jnp.broadcast_to(scale_of(codes), (128, 256)))[:, :1]
    guided = kept_ref[...] + back_ref[:256].astype(jnp.float32) * scale
    peak = jnp.max(guided, axis=1, keepdims=True)
    expo = jnp.exp(guided - peak)
    total = jnp.sum(expo, axis=1, keepdims=True)
    moment = jnp.sum(expo * guided, axis=1, keepdims=True)
    lane = lax.broadcasted_iota(jnp.int32, (256, 128), 1)
    table = jnp.transpose(jnp.where(lane == 0, peak + jnp.log(total), moment / total))
    rows = [table[i : i + 1, at : at + 128] for i in (0, 1) for at in (0, 128)]
    tile = jnp.concatenate(rows + [jnp.zeros((4, 128), jnp.float32)], 0)
    stats_ref[...] = jnp.broadcast_to(tile[None], (64, 8, 128))
    guided_ref[...] = guided


def join(kept, back):
    return pl.pallas_call(
        join_kernel,
        out_shape=(
            jax.ShapeDtypeStruct(kept.shape, jnp.float32),
            jax.ShapeDtypeStruct((64, 8, 128), jnp.float32),
        ),
        in_specs=in_vmem(2),
        out_specs=in_vmem(2),
        compiler_params=room(12),
        name="join",
    )(kept, back)


def local(hidden, head, scale_index, threshold):
    core, far = lax.axis_index("cfg"), lax.axis_index("zh")
    y, x, zl = lax.axis_index("y"), lax.axis_index("x"), lax.axis_index("zl")
    slot = jnp.arange(8)
    place = jnp.zeros((8,), jnp.int32)
    for i, at in enumerate((core, far, y, x, zl)):
        place = jnp.where(slot == i, at, place)
    features = hidden[0].T
    other = lax.ppermute(features, "cfg", [(0, 1), (1, 0)])
    away_scale = lax.ppermute(scale_index, ("zl", "zh"), pairs(("zl", "zh"), nearest_other))
    limits = lax.dynamic_slice_in_dim(threshold, core * 256, 256, 0).astype(jnp.float32) / 8.0

    own, own_scale = load(features, scale_index[None])
    away, home = mix(place, own, other, own_scale, away_scale[None])
    (head,) = load(lax.optimization_barrier((head, away))[0])

    def near(block):
        return [block] + [shifted(block, "zl", k) for k in (1, 2, 3)]

    def spread(block, first, second):
        return [block] + [crossed(block, first, second, k) for k in (1, 2, 3)]

    away_near = near(away)
    home_near = near(home)
    away_column = stack(place, away_near, (head,))
    away_line = spread(away_column, "x", "y")
    home_column = stack(place, home_near, (away_column,))
    home_line = spread(home_column, "x", "y")
    away_parts = spread(pack(away_line, (home_near[1],home_near[2])), "y", "x")
    sent = product(place, head, away_parts, False, ())
    back = lax.ppermute(sent, "zh", [(0, 1), (1, 0)])
    home_parts = spread(pack(home_line, (away_parts[1], away_parts[3])), "y", "x")
    kept = product(place, head, home_parts, True, ())

    guided, stats = join(kept, back)
    stats = lax.all_to_all(stats, ("y", "x", "zl"), 0, 0, tiled=True)
    each, mean = stats[:, :2], stats[:, 2:4]
    top = jnp.max(each, axis=0)
    weight = jnp.exp(each - top)
    total = jnp.sum(weight, axis=0)
    lse = top + jnp.log(total)
    entropy = lse - jnp.sum(weight * mean, axis=0) / total
    lse, entropy = lse.reshape(256), entropy.reshape(256)
    logprob = guided - lse[:, None]
    deviation = -logprob - entropy[:, None]
    typical = jax.nn.sigmoid(2.0 * (limits[:, None] - jnp.abs(deviation)))
    return logprob.astype(jnp.bfloat16), typical.astype(jnp.bfloat16), entropy


def solution(mesh):
    torus = Mesh(mesh.devices.reshape(SIZES), AXES)
    vocab = ("y", "x", "zl")
    return jax.shard_map(
        local,
        mesh=torus,
        in_specs=(P("cfg", None, ("zh", *vocab)), P("zh", vocab), P("zh"), P("zh")),
        out_specs=(P(("zh", "cfg"), vocab), P(("zh", "cfg"), vocab), P(("zh", "cfg"))),
        check_vma=False,
    )
```

```python
import math

import jax
import jax.numpy as jnp
from jax import lax
from jax.experimental import pallas as pl
from jax.experimental.pallas import tpu as pltpu
from jax.sharding import Mesh, PartitionSpec as P

AXES = ("cfg", "y", "x", "zl", "zh")
SIZES = (2, 4, 4, 4, 2)
TOP = 32767.0
STEP = math.log(2.0) / 256.0


def pairs(axes, move):
    dims = [SIZES[AXES.index(a)] for a in axes]
    route = []
    for i in range(math.prod(dims)):
        rest, at = i, {}
        for a, n in reversed(list(zip(axes, dims))):
            at[a], rest = rest % n, rest // n
        to = move(dict(at))
        j = 0
        for a, n in zip(axes, dims):
            j = j * n + to[a] % n
        route.append((i, j))
    return route


def shifted(block, axis, k):
    return lax.ppermute(block, axis, pairs((axis,), lambda at: {axis: at[axis] + k}))


def crossed(block, first, second, k):
    def move(at):
        along = first if at["cfg"] == 0 else second
        at[along] += k
        return at

    axes = ("cfg", "y", "x")
    return lax.ppermute(block, axes, pairs(axes, move))


def nearest_other(at):
    z = at["zh"] * 4 + at["zl"]
    z = (z + (2 if z % 4 >= 2 else 6)) % 8
    return {"zh": z // 4, "zl": z % 4}


def code_of(largest):
    return jnp.ceil(jnp.log(jnp.maximum(largest, 1e-30)) * (1.0 / STEP)) + 1.0


def scale_of(code):
    return jnp.exp(code * STEP) * (1.0 / TOP)


def coded(values, scale):
    return jnp.clip(jnp.round(values / scale), -TOP, TOP).astype(jnp.int32).astype(jnp.int16)


def in_vmem(count):
    return [pl.BlockSpec(memory_space=pltpu.VMEM)] * count


def anywhere(arrays):
    return [pl.BlockSpec(memory_space=pl.ANY)] * len(arrays)


def room(mib):
    return pltpu.CompilerParams(vmem_limit_bytes=mib << 20)


def load_kernel(*refs):
    count = len(refs) // 2
    copies = [pltpu.make_async_copy(refs[i], refs[count + i], refs[-1].at[i]) for i in range(count)]
    for copy in copies:
        copy.start()
    for copy in copies:
        copy.wait()


def load(*arrays):
    return pl.pallas_call(
        load_kernel,
        out_shape=[jax.ShapeDtypeStruct(a.shape, a.dtype) for a in arrays],
        in_specs=anywhere(arrays),
        out_specs=in_vmem(len(arrays)),
        scratch_shapes=[pltpu.SemaphoreType.DMA((len(arrays),))],
        compiler_params=room(44),
        cost_estimate=pl.CostEstimate(
            flops=0, bytes_accessed=2 * sum(a.size * a.dtype.itemsize for a in arrays), transcendentals=0
        ),
        name="load",
    )(*arrays)


def mix_kernel(place_ref, own_ref, other_ref, own_scale_ref, away_scale_ref, *out_refs):
    core, far = place_ref[0], place_ref[1]
    first = core == 0
    for n, half in enumerate((1 - far, far)):
        cut = pl.ds(pl.multiple_of(half * 512 + core * 256, 256), 256)
        scale_ref = away_scale_ref if n == 0 else own_scale_ref
        scales = scale_ref[:, pl.ds(pl.multiple_of(core * 256, 256), 256)]
        guide = 1.0 + 0.5 * scales.astype(jnp.float32)
        own = own_ref[:, cut].astype(jnp.float32)
        other = other_ref[:, cut].astype(jnp.float32)
        cond = jnp.where(first, own, other)
        uncond = jnp.where(first, other, own)
        mixed = uncond + guide * (cond - uncond)
        code = code_of(jnp.max(jnp.abs(mixed), axis=0, keepdims=True))
        out_refs[n][:64] = coded(mixed, scale_of(code))
        out_refs[n][64:] = jnp.broadcast_to(code, (16, 256)).astype(jnp.int32).astype(jnp.int16)


def mix(place, own, other, own_scale, away_scale):
    return pl.pallas_call(
        mix_kernel,
        out_shape=[jax.ShapeDtypeStruct((80, 256), jnp.int16)] * 2,
        in_specs=[pl.BlockSpec(memory_space=pltpu.SMEM)] + in_vmem(4),
        out_specs=in_vmem(2),
        compiler_params=room(4),
        name="mix",
    )(place, own, other, own_scale, away_scale)


def hold_kernel(block_ref, *refs):
    refs[-1][...] = block_ref[...]


def hold(block, after):
    return pl.pallas_call(
        hold_kernel,
        out_shape=jax.ShapeDtypeStruct(block.shape, block.dtype),
        in_specs=in_vmem(1) + anywhere(after),
        out_specs=in_vmem(1)[0],
        compiler_params=room(4),
        name="hold",
    )(block, *after)


def stack_kernel(place_ref, a_ref, b_ref, c_ref, d_ref, *refs):
    out_ref = refs[-1]
    width = a_ref.shape[1]
    row = lax.broadcasted_iota(jnp.int32, (16, width), 0)
    codes = jnp.zeros((16, width), jnp.int32)
    for k, ref in enumerate((a_ref, b_ref, c_ref, d_ref)):
        place = (place_ref[4] - k) & 3
        out_ref[pl.ds(pl.multiple_of(place * 64, 64), 64), :] = ref[:64]
        codes = jnp.where(row & 3 == place, ref[64:].astype(jnp.int32), codes)
    out_ref[256:] = codes.astype(jnp.int16)


def stack(place, parts, after):
    return pl.pallas_call(
        stack_kernel,
        out_shape=jax.ShapeDtypeStruct((272, parts[0].shape[1]), jnp.int16),
        in_specs=[pl.BlockSpec(memory_space=pltpu.SMEM)] + in_vmem(4) + anywhere(after),
        out_specs=in_vmem(1)[0],
        compiler_params=room(4),
        name="stack",
    )(place, *parts, *after)


def pack_kernel(*refs):
    out_ref = refs[-1]
    row = lax.broadcasted_iota(jnp.int32, (16, out_ref.shape[1]), 0)
    codes = jnp.zeros(row.shape, jnp.int32)
    for k in range(4):
        out_ref[256 * k : 256 * k + 256] = refs[k][:256]
        codes = jnp.where(row >> 2 == k, refs[k][256:].astype(jnp.int32), codes)
    out_ref[1024:] = codes.astype(jnp.int16)


def pack(line, after):
    return pl.pallas_call(
        pack_kernel,
        out_shape=jax.ShapeDtypeStruct((1040, line[0].shape[1]), jnp.int16),
        in_specs=in_vmem(4) + anywhere(after),
        out_specs=in_vmem(1)[0],
        compiler_params=room(4),
        name="pack",
    )(*line, *after)


def product_kernel(place_ref, head_ref, *refs):
    parts, out_ref, total_ref = refs[:4], refs[-2], refs[-1]
    core, y, x = place_ref[0], place_ref[2], place_ref[3]
    count = total_ref.shape[0] // 2
    dims = (((0,), (0,)), ((), ()))
    for k, part in enumerate(parts):
        total = None
        scale = scale_of(part[1024:].astype(jnp.float32))
        for piece in range(4):
            high, low = [], []
            for j in range(4):
                at = 4 * piece + j
                values = part[64 * at : 64 * at + 64].astype(jnp.float32) * scale[at : at + 1]
                top = values.astype(jnp.bfloat16)
                high.append(top)
                low.append((values - top.astype(jnp.float32)).astype(jnp.bfloat16))
            both = jnp.concatenate([jnp.concatenate(high, 0), jnp.concatenate(low, 0)], 1)
            row = jnp.where(core == 0, y - k, y - piece) & 3
            column = jnp.where(core == 0, x - piece, x - k) & 3
            weight = head_ref[pl.ds(pl.multiple_of((row * 4 + column) * 256, 256), 256), :]
            term = lax.dot_general(both, weight, dims, preferred_element_type=jnp.float32)
            total = term if total is None else total + term
        if k == 0:
            total_ref[...] = total
        else:
            total_ref[...] += total
    total = total_ref[:count] + total_ref[count:]
    if out_ref.dtype == jnp.float32:
        out_ref[...] = total
    else:
        code = code_of(jnp.max(jnp.abs(total), axis=1, keepdims=True))
        out_ref[:count] = coded(total, scale_of(code))
        across = jnp.transpose(jnp.broadcast_to(code, (count, 128)))[:16]
        out_ref[count:] = jnp.zeros((16, total.shape[1]), jnp.int16)
        out_ref[count:, :count] = across.astype(jnp.int32).astype(jnp.int16)


def product(place, head, parts, keep, after):
    tokens, width = parts[0].shape[1], head.shape[1]
    out = (
        jax.ShapeDtypeStruct((tokens, width), jnp.float32)
        if keep
        else jax.ShapeDtypeStruct((tokens + 16, width), jnp.int16)
    )
    return pl.pallas_call(
        product_kernel,
        out_shape=out,
        in_specs=[pl.BlockSpec(memory_space=pltpu.SMEM)] + in_vmem(5) + anywhere(after),
        out_specs=in_vmem(1)[0],
        scratch_shapes=[pltpu.VMEM((2 * tokens, width), jnp.float32)],
        compiler_params=room(24),
        cost_estimate=pl.CostEstimate(
            flops=0 if keep else 4 * tokens * 4096 * width, bytes_accessed=0, transcendentals=0
        ),
        name="product",
    )(place, head, *parts, *after)


def join_kernel(kept_ref, back_ref, guided_ref, stats_ref):
    codes = back_ref[256:, :256].astype(jnp.float32)[:1]
    scale = jnp.transpose(jnp.broadcast_to(scale_of(codes), (128, 256)))[:, :1]
    guided = kept_ref[...] + back_ref[:256].astype(jnp.float32) * scale
    peak = jnp.max(guided, axis=1, keepdims=True)
    expo = jnp.exp(guided - peak)
    total = jnp.sum(expo, axis=1, keepdims=True)
    moment = jnp.sum(expo * guided, axis=1, keepdims=True)
    lane = lax.broadcasted_iota(jnp.int32, (256, 128), 1)
    table = jnp.transpose(jnp.where(lane == 0, peak + jnp.log(total), moment / total))
    rows = [table[i : i + 1, at : at + 128] for i in (0, 1) for at in (0, 128)]
    tile = jnp.concatenate(rows + [jnp.zeros((4, 128), jnp.float32)], 0)
    stats_ref[...] = jnp.broadcast_to(tile[None], (64, 8, 128))
    guided_ref[...] = guided


def join(kept, back):
    return pl.pallas_call(
        join_kernel,
        out_shape=(
            jax.ShapeDtypeStruct(kept.shape, jnp.float32),
            jax.ShapeDtypeStruct((64, 8, 128), jnp.float32),
        ),
        in_specs=in_vmem(2),
        out_specs=in_vmem(2),
        compiler_params=room(12),
        name="join",
    )(kept, back)


def local(hidden, head, scale_index, threshold):
    core, far = lax.axis_index("cfg"), lax.axis_index("zh")
    y, x, zl = lax.axis_index("y"), lax.axis_index("x"), lax.axis_index("zl")
    slot = jnp.arange(8)
    place = jnp.zeros((8,), jnp.int32)
    for i, at in enumerate((core, far, y, x, zl)):
        place = jnp.where(slot == i, at, place)
    features = hidden[0].T
    other = lax.ppermute(features, "cfg", [(0, 1), (1, 0)])
    away_scale = lax.ppermute(scale_index, ("zl", "zh"), pairs(("zl", "zh"), nearest_other))
    limits = lax.dynamic_slice_in_dim(threshold, core * 256, 256, 0).astype(jnp.float32) / 8.0

    own, own_scale = load(features, scale_index[None])
    away, home = mix(place, own, other, own_scale, away_scale[None])
    (head,) = load(lax.optimization_barrier((head, away))[0])

    def near(block):
        return [block] + [shifted(block, "zl", k) for k in (1, 2, 3)]

    def spread(block, first, second):
        return [block] + [crossed(block, first, second, k) for k in (1, 2, 3)]

    away_near = near(away)
    home_near = near(hold(home, away_near[1:]))
    away_line = spread(stack(place, away_near, (head,)), "x", "y")
    away_block = pack(away_line, ())
    away_parts = spread(away_block, "y", "x")
    home_line = spread(stack(place, home_near, (away_block,)), "x", "y")
    sent = product(place, head, away_parts, False, ())
    back = lax.ppermute(sent, "zh", [(0, 1), (1, 0)])
    home_parts = spread(pack(home_line, (sent,)), "y", "x")
    kept = product(place, head, home_parts, True, ())

    guided, stats = join(kept, back)
    stats = lax.all_to_all(stats, ("y", "x", "zl"), 0, 0, tiled=True)
    each, mean = stats[:, :2], stats[:, 2:4]
    top = jnp.max(each, axis=0)
    weight = jnp.exp(each - top)
    total = jnp.sum(weight, axis=0)
    lse = top + jnp.log(total)
    entropy = lse - jnp.sum(weight * mean, axis=0) / total
    lse, entropy = lse.reshape(256), entropy.reshape(256)
    logprob = guided - lse[:, None]
    deviation = -logprob - entropy[:, None]
    typical = jax.nn.sigmoid(2.0 * (limits[:, None] - jnp.abs(deviation)))
    return logprob.astype(jnp.bfloat16), typical.astype(jnp.bfloat16), entropy


def solution(mesh):
    torus = Mesh(mesh.devices.reshape(SIZES), AXES)
    vocab = ("y", "x", "zl")
    return jax.shard_map(
        local,
        mesh=torus,
        in_specs=(P("cfg", None, ("zh", *vocab)), P("zh", vocab), P("zh"), P("zh")),
        out_specs=(P(("zh", "cfg"), vocab), P(("zh", "cfg"), vocab), P(("zh", "cfg"))),
        check_vma=False,
    )
```

```python
import functools
import math

import jax
import jax.numpy as jnp
from jax import lax
from jax.experimental import pallas as pl
from jax.experimental.pallas import tpu as pltpu
from jax.sharding import Mesh, PartitionSpec as P

AXES = ("cfg", "y", "x", "zl", "zh")
SIZES = (2, 4, 4, 4, 2)
TOP = 32767.0
STEP = math.log(2.0) / 256.0


def pairs(axes, move):
    dims = [SIZES[AXES.index(a)] for a in axes]
    route = []
    for i in range(math.prod(dims)):
        rest, at = i, {}
        for a, n in reversed(list(zip(axes, dims))):
            at[a], rest = rest % n, rest // n
        to = move(dict(at))
        j = 0
        for a, n in zip(axes, dims):
            j = j * n + to[a] % n
        route.append((i, j))
    return route


def shifted(block, axis, k):
    return lax.ppermute(block, axis, pairs((axis,), lambda at: {axis: at[axis] + k}))


def crossed(block, first, second, k):
    def move(at):
        along = first if at["cfg"] == 0 else second
        at[along] += k
        return at

    axes = ("cfg", "y", "x")
    return lax.ppermute(block, axes, pairs(axes, move))


def nearest_other(at):
    z = at["zh"] * 4 + at["zl"]
    z = (z + (2 if z % 4 >= 2 else 6)) % 8
    return {"zh": z // 4, "zl": z % 4}


def code_of(largest):
    return jnp.ceil(jnp.log(jnp.maximum(largest, 1e-30)) * (1.0 / STEP)) + 1.0


def scale_of(code):
    return jnp.exp(code * STEP) * (1.0 / TOP)


def coded(values, scale):
    return jnp.clip(jnp.round(values / scale), -TOP, TOP).astype(jnp.int32).astype(jnp.int16)


def in_vmem(count):
    return [pl.BlockSpec(memory_space=pltpu.VMEM)] * count


def anywhere(arrays):
    return [pl.BlockSpec(memory_space=pl.ANY)] * len(arrays)


def room(mib):
    return pltpu.CompilerParams(vmem_limit_bytes=mib << 20)


def load_kernel(*refs):
    count = len(refs) // 2
    copies = [pltpu.make_async_copy(refs[i], refs[count + i], refs[-1].at[i]) for i in range(count)]
    for copy in copies:
        copy.start()
    for copy in copies:
        copy.wait()


def load(*arrays):
    return pl.pallas_call(
        load_kernel,
        out_shape=[jax.ShapeDtypeStruct(a.shape, a.dtype) for a in arrays],
        in_specs=anywhere(arrays),
        out_specs=in_vmem(len(arrays)),
        scratch_shapes=[pltpu.SemaphoreType.DMA((len(arrays),))],
        compiler_params=room(44),
        cost_estimate=pl.CostEstimate(
            flops=0, bytes_accessed=2 * sum(a.size * a.dtype.itemsize for a in arrays), transcendentals=0
        ),
        name="load",
    )(*arrays)


def mix_kernel(place_ref, own_ref, other_ref, own_scale_ref, away_scale_ref, *out_refs):
    core, far = place_ref[0], place_ref[1]
    first = core == 0
    for n, half in enumerate((1 - far, far)):
        cut = pl.ds(pl.multiple_of(half * 512 + core * 256, 256), 256)
        scale_ref = away_scale_ref if n == 0 else own_scale_ref
        scales = scale_ref[:, pl.ds(pl.multiple_of(core * 256, 256), 256)]
        guide = 1.0 + 0.5 * scales.astype(jnp.float32)
        own = own_ref[:, cut].astype(jnp.float32)
        other = other_ref[:, cut].astype(jnp.float32)
        cond = jnp.where(first, own, other)
        uncond = jnp.where(first, other, own)
        mixed = uncond + guide * (cond - uncond)
        code = code_of(jnp.max(jnp.abs(mixed), axis=0, keepdims=True))
        out_refs[n][:64] = coded(mixed, scale_of(code))
        out_refs[n][64:] = jnp.broadcast_to(code, (16, 256)).astype(jnp.int32).astype(jnp.int16)


def mix(place, own, other, own_scale, away_scale):
    return pl.pallas_call(
        mix_kernel,
        out_shape=[jax.ShapeDtypeStruct((80, 256), jnp.int16)] * 2,
        in_specs=[pl.BlockSpec(memory_space=pltpu.SMEM)] + in_vmem(4),
        out_specs=in_vmem(2),
        compiler_params=room(4),
        name="mix",
    )(place, own, other, own_scale, away_scale)


def hold_kernel(block_ref, *refs):
    refs[-1][...] = block_ref[...]


def hold(block, after):
    return pl.pallas_call(
        hold_kernel,
        out_shape=jax.ShapeDtypeStruct(block.shape, block.dtype),
        in_specs=in_vmem(1) + anywhere(after),
        out_specs=in_vmem(1)[0],
        compiler_params=room(4),
        name="hold",
    )(block, *after)


def stack_kernel(place_ref, a_ref, b_ref, c_ref, d_ref, *refs):
    out_ref = refs[-1]
    width = a_ref.shape[1]
    row = lax.broadcasted_iota(jnp.int32, (16, width), 0)
    codes = jnp.zeros((16, width), jnp.int32)
    for k, ref in enumerate((a_ref, b_ref, c_ref, d_ref)):
        place = (place_ref[4] - k) & 3
        out_ref[pl.ds(pl.multiple_of(place * 64, 64), 64), :] = ref[:64]
        codes = jnp.where(row & 3 == place, ref[64:].astype(jnp.int32), codes)
    out_ref[256:] = codes.astype(jnp.int16)


def stack(place, parts, after):
    return pl.pallas_call(
        stack_kernel,
        out_shape=jax.ShapeDtypeStruct((272, parts[0].shape[1]), jnp.int16),
        in_specs=[pl.BlockSpec(memory_space=pltpu.SMEM)] + in_vmem(4) + anywhere(after),
        out_specs=in_vmem(1)[0],
        compiler_params=room(4),
        name="stack",
    )(place, *parts, *after)


def pack_kernel(*refs):
    out_ref = refs[-1]
    row = lax.broadcasted_iota(jnp.int32, (16, out_ref.shape[1]), 0)
    codes = jnp.zeros(row.shape, jnp.int32)
    for k in range(4):
        out_ref[256 * k : 256 * k + 256] = refs[k][:256]
        codes = jnp.where(row >> 2 == k, refs[k][256:].astype(jnp.int32), codes)
    out_ref[1024:] = codes.astype(jnp.int16)


def pack(line, after):
    return pl.pallas_call(
        pack_kernel,
        out_shape=jax.ShapeDtypeStruct((1040, line[0].shape[1]), jnp.int16),
        in_specs=in_vmem(4) + anywhere(after),
        out_specs=in_vmem(1)[0],
        compiler_params=room(4),
        name="pack",
    )(*line, *after)


def product_kernel(offsets, adds, place_ref, head_ref, *refs):
    parts, out_ref, total_ref = refs[: len(offsets)], refs[-2], refs[-1]
    core, y, x = place_ref[0], place_ref[2], place_ref[3]
    count = total_ref.shape[0] // 2
    dims = (((0,), (0,)), ((), ()))
    for i, (k, part) in enumerate(zip(offsets, parts)):
        total = None
        scale = scale_of(part[1024:].astype(jnp.float32))
        for piece in range(4):
            high, low = [], []
            for j in range(4):
                at = 4 * piece + j
                values = part[64 * at : 64 * at + 64].astype(jnp.float32) * scale[at : at + 1]
                top = values.astype(jnp.bfloat16)
                high.append(top)
                low.append((values - top.astype(jnp.float32)).astype(jnp.bfloat16))
            both = jnp.concatenate([jnp.concatenate(high, 0), jnp.concatenate(low, 0)], 1)
            row = jnp.where(core == 0, y - k, y - piece) & 3
            column = jnp.where(core == 0, x - piece, x - k) & 3
            weight = head_ref[pl.ds(pl.multiple_of((row * 4 + column) * 256, 256), 256), :]
            term = lax.dot_general(both, weight, dims, preferred_element_type=jnp.float32)
            total = term if total is None else total + term
        if i == 0:
            total_ref[...] = total
        else:
            total_ref[...] += total
    total = total_ref[:count] + total_ref[count:]
    if adds:
        total += refs[len(offsets)][...]
    if out_ref.dtype == jnp.float32:
        out_ref[...] = total
    else:
        code = code_of(jnp.max(jnp.abs(total), axis=1, keepdims=True))
        out_ref[:count] = coded(total, scale_of(code))
        across = jnp.transpose(jnp.broadcast_to(code, (count, 128)))[:16]
        out_ref[count:] = jnp.zeros((16, total.shape[1]), jnp.int16)
        out_ref[count:, :count] = across.astype(jnp.int32).astype(jnp.int16)


def product(place, head, parts, offsets, before=(), send=False, cost=0):
    chosen = [parts[k] for k in offsets]
    tokens, width = chosen[0].shape[1], head.shape[1]
    out = (
        jax.ShapeDtypeStruct((tokens + 16, width), jnp.int16)
        if send
        else jax.ShapeDtypeStruct((tokens, width), jnp.float32)
    )
    return pl.pallas_call(
        functools.partial(product_kernel, offsets, len(before) > 0),
        out_shape=out,
        in_specs=[pl.BlockSpec(memory_space=pltpu.SMEM)] + in_vmem(1 + len(chosen) + len(before)),
        out_specs=in_vmem(1)[0],
        scratch_shapes=[pltpu.VMEM((2 * tokens, width), jnp.float32)],
        compiler_params=room(24),
        cost_estimate=pl.CostEstimate(
            flops=cost * len(offsets) * tokens * 4096 * width, bytes_accessed=0, transcendentals=0
        ),
        name="product",
    )(place, head, *chosen, *before)


def join_kernel(kept_ref, back_ref, guided_ref, stats_ref):
    codes = back_ref[256:, :256].astype(jnp.float32)[:1]
    scale = jnp.transpose(jnp.broadcast_to(scale_of(codes), (128, 256)))[:, :1]
    guided = kept_ref[...] + back_ref[:256].astype(jnp.float32) * scale
    peak = jnp.max(guided, axis=1, keepdims=True)
    expo = jnp.exp(guided - peak)
    total = jnp.sum(expo, axis=1, keepdims=True)
    moment = jnp.sum(expo * guided, axis=1, keepdims=True)
    lane = lax.broadcasted_iota(jnp.int32, (256, 128), 1)
    table = jnp.transpose(jnp.where(lane == 0, peak + jnp.log(total), moment / total))
    rows = [table[i : i + 1, at : at + 128] for i in (0, 1) for at in (0, 128)]
    tile = jnp.concatenate(rows + [jnp.zeros((4, 128), jnp.float32)], 0)
    stats_ref[...] = jnp.broadcast_to(tile[None], (64, 8, 128))
    guided_ref[...] = guided


def join(kept, back):
    return pl.pallas_call(
        join_kernel,
        out_shape=(
            jax.ShapeDtypeStruct(kept.shape, jnp.float32),
            jax.ShapeDtypeStruct((64, 8, 128), jnp.float32),
        ),
        in_specs=in_vmem(2),
        out_specs=in_vmem(2),
        compiler_params=room(12),
        name="join",
    )(kept, back)


def local(hidden, head, scale_index, threshold):
    core, far = lax.axis_index("cfg"), lax.axis_index("zh")
    y, x, zl = lax.axis_index("y"), lax.axis_index("x"), lax.axis_index("zl")
    slot = jnp.arange(8)
    place = jnp.zeros((8,), jnp.int32)
    for i, at in enumerate((core, far, y, x, zl)):
        place = jnp.where(slot == i, at, place)
    features = hidden[0].T
    other = lax.ppermute(features, "cfg", [(0, 1), (1, 0)])
    away_scale = lax.ppermute(scale_index, ("zl", "zh"), pairs(("zl", "zh"), nearest_other))
    limits = lax.dynamic_slice_in_dim(threshold, core * 256, 256, 0).astype(jnp.float32) / 8.0

    own, own_scale = load(features, scale_index[None])
    away, home = mix(place, own, other, own_scale, away_scale[None])
    (head,) = load(lax.optimization_barrier((head, away))[0])

    def near(block):
        return [block] + [shifted(block, "zl", k) for k in (1, 2, 3)]

    def spread(block, first, second):
        return [block] + [crossed(block, first, second, k) for k in (1, 2, 3)]

    away_near = near(away)
    home_near = near(hold(home, away_near[1:]))
    away_line = spread(stack(place, away_near, (head,)), "x", "y")
    away_block = pack(away_line, ())
    away_parts = spread(away_block, "y", "x")
    home_line = spread(stack(place, home_near, (away_block,)), "x", "y")
    away_sum = product(place, head, away_parts, (0,), cost=1)
    away_sum = product(place, head, away_parts, (1,), (away_sum,), cost=1)
    sent = product(place, head, away_parts, (2, 3), (away_sum,), True, cost=1)
    back = lax.ppermute(sent, "zh", [(0, 1), (1, 0)])
    home_parts = spread(pack(home_line, (sent,)), "y", "x")
    kept = product(place, head, home_parts, (0, 1))
    kept = product(place, head, home_parts, (2,), (kept,))
    kept = product(place, head, home_parts, (3,), (kept,))

    guided, stats = join(kept, back)
    stats = lax.all_to_all(stats, ("y", "x", "zl"), 0, 0, tiled=True)
    each, mean = stats[:, :2], stats[:, 2:4]
    top = jnp.max(each, axis=0)
    weight = jnp.exp(each - top)
    total = jnp.sum(weight, axis=0)
    lse = top + jnp.log(total)
    entropy = lse - jnp.sum(weight * mean, axis=0) / total
    lse, entropy = lse.reshape(256), entropy.reshape(256)
    logprob = guided - lse[:, None]
    deviation = -logprob - entropy[:, None]
    typical = jax.nn.sigmoid(2.0 * (limits[:, None] - jnp.abs(deviation)))
    return logprob.astype(jnp.bfloat16), typical.astype(jnp.bfloat16), entropy


def solution(mesh):
    torus = Mesh(mesh.devices.reshape(SIZES), AXES)
    vocab = ("y", "x", "zl")
    return jax.shard_map(
        local,
        mesh=torus,
        in_specs=(P("cfg", None, ("zh", *vocab)), P("zh", vocab), P("zh"), P("zh")),
        out_specs=(P(("zh", "cfg"), vocab), P(("zh", "cfg"), vocab), P(("zh", "cfg"))),
        check_vma=False,
    )
```

```python
import functools
import math

import jax
import jax.numpy as jnp
from jax import lax
from jax.experimental import pallas as pl
from jax.experimental.pallas import tpu as pltpu
from jax.sharding import Mesh, PartitionSpec as P

AXES = ("cfg", "y", "x", "zl", "zh")
SIZES = (2, 4, 4, 4, 2)
TOP = 32767.0
STEP = math.log(2.0) / 256.0


def pairs(axes, move):
    dims = [SIZES[AXES.index(a)] for a in axes]
    route = []
    for i in range(math.prod(dims)):
        rest, at = i, {}
        for a, n in reversed(list(zip(axes, dims))):
            at[a], rest = rest % n, rest // n
        to = move(dict(at))
        j = 0
        for a, n in zip(axes, dims):
            j = j * n + to[a] % n
        route.append((i, j))
    return route


def shifted(block, axis, k):
    return lax.ppermute(block, axis, pairs((axis,), lambda at: {axis: at[axis] + k}))


def crossed(block, first, second, k):
    def move(at):
        along = first if at["cfg"] == 0 else second
        at[along] += k
        return at

    axes = ("cfg", "y", "x")
    return lax.ppermute(block, axes, pairs(axes, move))


def nearest_other(at):
    z = at["zh"] * 4 + at["zl"]
    z = (z + (2 if z % 4 >= 2 else 6)) % 8
    return {"zh": z // 4, "zl": z % 4}


def code_of(largest):
    return jnp.ceil(jnp.log(jnp.maximum(largest, 1e-30)) * (1.0 / STEP)) + 1.0


def scale_of(code):
    return jnp.exp(code * STEP) * (1.0 / TOP)


def coded(values, scale):
    return jnp.clip(jnp.round(values / scale), -TOP, TOP).astype(jnp.int32).astype(jnp.int16)


def in_vmem(count):
    return [pl.BlockSpec(memory_space=pltpu.VMEM)] * count


def anywhere(arrays):
    return [pl.BlockSpec(memory_space=pl.ANY)] * len(arrays)


def room(mib):
    return pltpu.CompilerParams(vmem_limit_bytes=mib << 20)


def load_kernel(*refs):
    count = len(refs) // 2
    copies = [pltpu.make_async_copy(refs[i], refs[count + i], refs[-1].at[i]) for i in range(count)]
    for copy in copies:
        copy.start()
    for copy in copies:
        copy.wait()


def load(*arrays):
    return pl.pallas_call(
        load_kernel,
        out_shape=[jax.ShapeDtypeStruct(a.shape, a.dtype) for a in arrays],
        in_specs=anywhere(arrays),
        out_specs=in_vmem(len(arrays)),
        scratch_shapes=[pltpu.SemaphoreType.DMA((len(arrays),))],
        compiler_params=room(44),
        cost_estimate=pl.CostEstimate(
            flops=0, bytes_accessed=2 * sum(a.size * a.dtype.itemsize for a in arrays), transcendentals=0
        ),
        name="load",
    )(*arrays)


def mix_kernel(place_ref, own_ref, other_ref, own_scale_ref, away_scale_ref, *out_refs):
    core, far = place_ref[0], place_ref[1]
    first = core == 0
    for n, half in enumerate((1 - far, far)):
        cut = pl.ds(pl.multiple_of(half * 512 + core * 256, 256), 256)
        scale_ref = away_scale_ref if n == 0 else own_scale_ref
        scales = scale_ref[:, pl.ds(pl.multiple_of(core * 256, 256), 256)]
        guide = 1.0 + 0.5 * scales.astype(jnp.float32)
        own = own_ref[:, cut].astype(jnp.float32)
        other = other_ref[:, cut].astype(jnp.float32)
        cond = jnp.where(first, own, other)
        uncond = jnp.where(first, other, own)
        mixed = uncond + guide * (cond - uncond)
        code = code_of(jnp.max(jnp.abs(mixed), axis=0, keepdims=True))
        out_refs[n][:64] = coded(mixed, scale_of(code))
        out_refs[n][64:] = jnp.broadcast_to(code, (16, 256)).astype(jnp.int32).astype(jnp.int16)


def mix(place, own, other, own_scale, away_scale):
    return pl.pallas_call(
        mix_kernel,
        out_shape=[jax.ShapeDtypeStruct((80, 256), jnp.int16)] * 2,
        in_specs=[pl.BlockSpec(memory_space=pltpu.SMEM)] + in_vmem(4),
        out_specs=in_vmem(2),
        compiler_params=room(4),
        name="mix",
    )(place, own, other, own_scale, away_scale)


def hold_kernel(block_ref, *refs):
    refs[-1][...] = block_ref[...]


def hold(block, after):
    return pl.pallas_call(
        hold_kernel,
        out_shape=jax.ShapeDtypeStruct(block.shape, block.dtype),
        in_specs=in_vmem(1) + anywhere(after),
        out_specs=in_vmem(1)[0],
        compiler_params=room(4),
        name="hold",
    )(block, *after)


def stack_kernel(place_ref, a_ref, b_ref, c_ref, d_ref, *refs):
    out_ref = refs[-1]
    width = a_ref.shape[1]
    row = lax.broadcasted_iota(jnp.int32, (16, width), 0)
    codes = jnp.zeros((16, width), jnp.int32)
    for k, ref in enumerate((a_ref, b_ref, c_ref, d_ref)):
        place = (place_ref[4] - k) & 3
        out_ref[pl.ds(pl.multiple_of(place * 64, 64), 64), :] = ref[:64]
        codes = jnp.where(row & 3 == place, ref[64:].astype(jnp.int32), codes)
    out_ref[256:] = codes.astype(jnp.int16)


def stack(place, parts, after):
    return pl.pallas_call(
        stack_kernel,
        out_shape=jax.ShapeDtypeStruct((272, parts[0].shape[1]), jnp.int16),
        in_specs=[pl.BlockSpec(memory_space=pltpu.SMEM)] + in_vmem(4) + anywhere(after),
        out_specs=in_vmem(1)[0],
        compiler_params=room(4),
        name="stack",
    )(place, *parts, *after)


def pack_kernel(*refs):
    out_ref = refs[-1]
    row = lax.broadcasted_iota(jnp.int32, (16, out_ref.shape[1]), 0)
    codes = jnp.zeros(row.shape, jnp.int32)
    for k in range(4):
        out_ref[256 * k : 256 * k + 256] = refs[k][:256]
        codes = jnp.where(row >> 2 == k, refs[k][256:].astype(jnp.int32), codes)
    out_ref[1024:] = codes.astype(jnp.int16)


def pack(line, after):
    return pl.pallas_call(
        pack_kernel,
        out_shape=jax.ShapeDtypeStruct((1040, line[0].shape[1]), jnp.int16),
        in_specs=in_vmem(4) + anywhere(after),
        out_specs=in_vmem(1)[0],
        compiler_params=room(4),
        name="pack",
    )(*line, *after)


def product_kernel(offsets, adds, place_ref, head_ref, *refs):
    parts, out_ref, total_ref = refs[: len(offsets)], refs[-2], refs[-1]
    core, y, x = place_ref[0], place_ref[2], place_ref[3]
    count = total_ref.shape[0] // 2
    dims = (((0,), (0,)), ((), ()))
    for i, (k, part) in enumerate(zip(offsets, parts)):
        total = None
        scale = scale_of(part[1024:].astype(jnp.float32))
        for piece in range(4):
            high, low = [], []
            for j in range(4):
                at = 4 * piece + j
                values = part[64 * at : 64 * at + 64].astype(jnp.float32) * scale[at : at + 1]
                top = values.astype(jnp.bfloat16)
                high.append(top)
                low.append((values - top.astype(jnp.float32)).astype(jnp.bfloat16))
            both = jnp.concatenate([jnp.concatenate(high, 0), jnp.concatenate(low, 0)], 1)
            row = jnp.where(core == 0, y - k, y - piece) & 3
            column = jnp.where(core == 0, x - piece, x - k) & 3
            weight = head_ref[pl.ds(pl.multiple_of((row * 4 + column) * 256, 256), 256), :]
            term = lax.dot_general(both, weight, dims, preferred_element_type=jnp.float32)
            total = term if total is None else total + term
        if i == 0:
            total_ref[...] = total
        else:
            total_ref[...] += total
    total = total_ref[:count] + total_ref[count:]
    if adds:
        total += refs[len(offsets)][...]
    if out_ref.dtype == jnp.float32:
        out_ref[...] = total
    else:
        code = code_of(jnp.max(jnp.abs(total), axis=1, keepdims=True))
        out_ref[:count] = coded(total, scale_of(code))
        across = jnp.transpose(jnp.broadcast_to(code, (count, 128)))[:16]
        out_ref[count:] = jnp.zeros((16, total.shape[1]), jnp.int16)
        out_ref[count:, :count] = across.astype(jnp.int32).astype(jnp.int16)


def product(place, head, parts, offsets, before=(), send=False, cost=0):
    chosen = [parts[k] for k in offsets]
    tokens, width = chosen[0].shape[1], head.shape[1]
    out = (
        jax.ShapeDtypeStruct((tokens + 16, width), jnp.int16)
        if send
        else jax.ShapeDtypeStruct((tokens, width), jnp.float32)
    )
    return pl.pallas_call(
        functools.partial(product_kernel, offsets, len(before) > 0),
        out_shape=out,
        in_specs=[pl.BlockSpec(memory_space=pltpu.SMEM)] + in_vmem(1 + len(chosen) + len(before)),
        out_specs=in_vmem(1)[0],
        scratch_shapes=[pltpu.VMEM((2 * tokens, width), jnp.float32)],
        compiler_params=room(24),
        cost_estimate=pl.CostEstimate(
            flops=cost * len(offsets) * tokens * 4096 * width, bytes_accessed=0, transcendentals=0
        ),
        name="product",
    )(place, head, *chosen, *before)


def join_kernel(kept_ref, back_ref, guided_ref, stats_ref):
    codes = back_ref[256:, :256].astype(jnp.float32)[:1]
    scale = jnp.transpose(jnp.broadcast_to(scale_of(codes), (128, 256)))[:, :1]
    guided = kept_ref[...] + back_ref[:256].astype(jnp.float32) * scale
    peak = jnp.max(guided, axis=1, keepdims=True)
    expo = jnp.exp(guided - peak)
    total = jnp.sum(expo, axis=1, keepdims=True)
    moment = jnp.sum(expo * guided, axis=1, keepdims=True)
    lane = lax.broadcasted_iota(jnp.int32, (256, 128), 1)
    table = jnp.transpose(jnp.where(lane == 0, peak + jnp.log(total), moment / total))
    rows = [table[i : i + 1, at : at + 128] for i in (0, 1) for at in (0, 128)]
    stats_ref[...] = jnp.broadcast_to(jnp.concatenate(rows, 0)[None], (64, 4, 128))
    guided_ref[...] = guided


def join(kept, back):
    return pl.pallas_call(
        join_kernel,
        out_shape=(
            jax.ShapeDtypeStruct(kept.shape, jnp.float32),
            jax.ShapeDtypeStruct((64, 4, 128), jnp.float32),
        ),
        in_specs=in_vmem(2),
        out_specs=in_vmem(2),
        compiler_params=room(12),
        name="join",
    )(kept, back)


def local(hidden, head, scale_index, threshold):
    core, far = lax.axis_index("cfg"), lax.axis_index("zh")
    y, x, zl = lax.axis_index("y"), lax.axis_index("x"), lax.axis_index("zl")
    slot = jnp.arange(8)
    place = jnp.zeros((8,), jnp.int32)
    for i, at in enumerate((core, far, y, x, zl)):
        place = jnp.where(slot == i, at, place)
    features = hidden[0].T
    other = lax.ppermute(features, "cfg", [(0, 1), (1, 0)])
    away_scale = lax.ppermute(scale_index, ("zl", "zh"), pairs(("zl", "zh"), nearest_other))
    limits = lax.dynamic_slice_in_dim(threshold, core * 256, 256, 0).astype(jnp.float32) / 8.0

    own, own_scale = load(features, scale_index[None])
    away, home = mix(place, own, other, own_scale, away_scale[None])
    (head,) = load(lax.optimization_barrier((head, away))[0])

    def near(block):
        return [block] + [shifted(block, "zl", k) for k in (1, 2, 3)]

    def spread(block, first, second):
        return [block] + [crossed(block, first, second, k) for k in (1, 2, 3)]

    away_near = near(away)
    away_line = spread(stack(place, away_near, ()), "x", "y")
    away_block = pack(away_line, (head,))
    away_parts = spread(away_block, "y", "x")
    away_sum = product(place, head, away_parts, (0,), cost=1)
    home_near = near(hold(home, (*away_near[1:], away_sum)))
    home_line = spread(stack(place, home_near, (away_block,)), "x", "y")
    sent = product(place, head, away_parts, (1, 2, 3), (away_sum,), True, cost=1)
    back = lax.ppermute(sent, "zh", [(0, 1), (1, 0)])
    home_parts = spread(pack(home_line, (sent,)), "y", "x")
    kept = product(place, head, home_parts, (0,))
    kept = product(place, head, home_parts, (1, 2, 3), (kept,))

    guided, stats = join(kept, back)
    stats = lax.all_to_all(stats, ("y", "x", "zl"), 0, 0, tiled=True)
    each, mean = stats[:, :2], stats[:, 2:4]
    top = jnp.max(each, axis=0)
    weight = jnp.exp(each - top)
    total = jnp.sum(weight, axis=0)
    lse = top + jnp.log(total)
    entropy = lse - jnp.sum(weight * mean, axis=0) / total
    lse, entropy = lse.reshape(256), entropy.reshape(256)
    logprob = guided - lse[:, None]
    deviation = -logprob - entropy[:, None]
    typical = jax.nn.sigmoid(2.0 * (limits[:, None] - jnp.abs(deviation)))
    return logprob.astype(jnp.bfloat16), typical.astype(jnp.bfloat16), entropy


def solution(mesh):
    torus = Mesh(mesh.devices.reshape(SIZES), AXES)
    vocab = ("y", "x", "zl")
    return jax.shard_map(
        local,
        mesh=torus,
        in_specs=(P("cfg", None, ("zh", *vocab)), P("zh", vocab), P("zh"), P("zh")),
        out_specs=(P(("zh", "cfg"), vocab), P(("zh", "cfg"), vocab), P(("zh", "cfg"))),
        check_vma=False,
    )
```

```python
import functools
import math

import jax
import jax.numpy as jnp
from jax import lax
from jax.experimental import pallas as pl
from jax.experimental.pallas import tpu as pltpu
from jax.sharding import Mesh, PartitionSpec as P

AXES = ("cfg", "y", "x", "zl", "zh")
SIZES = (2, 4, 4, 4, 2)
TOP = 32767.0
STEP = math.log(2.0) / 256.0


def pairs(axes, move):
    dims = [SIZES[AXES.index(a)] for a in axes]
    route = []
    for i in range(math.prod(dims)):
        rest, at = i, {}
        for a, n in reversed(list(zip(axes, dims))):
            at[a], rest = rest % n, rest // n
        to = move(dict(at))
        j = 0
        for a, n in zip(axes, dims):
            j = j * n + to[a] % n
        route.append((i, j))
    return route


def shifted(block, axis, k):
    return lax.ppermute(block, axis, pairs((axis,), lambda at: {axis: at[axis] + k}))


def crossed(block, first, second, k):
    def move(at):
        along = first if at["cfg"] == 0 else second
        at[along] += k
        return at

    axes = ("cfg", "y", "x")
    return lax.ppermute(block, axes, pairs(axes, move))


def nearest_other(at):
    z = at["zh"] * 4 + at["zl"]
    z = (z + (2 if z % 4 >= 2 else 6)) % 8
    return {"zh": z // 4, "zl": z % 4}


def code_of(largest):
    return jnp.ceil(jnp.log(jnp.maximum(largest, 1e-30)) * (1.0 / STEP)) + 1.0


def scale_of(code):
    return jnp.exp(code * STEP) * (1.0 / TOP)


def coded(values, scale):
    return jnp.clip(jnp.round(values / scale), -TOP, TOP).astype(jnp.int32).astype(jnp.int16)


def in_vmem(count):
    return [pl.BlockSpec(memory_space=pltpu.VMEM)] * count


def anywhere(arrays):
    return [pl.BlockSpec(memory_space=pl.ANY)] * len(arrays)


def room(mib):
    return pltpu.CompilerParams(vmem_limit_bytes=mib << 20)


def load_kernel(*refs):
    count = len(refs) // 2
    copies = [pltpu.make_async_copy(refs[i], refs[count + i], refs[-1].at[i]) for i in range(count)]
    for copy in copies:
        copy.start()
    for copy in copies:
        copy.wait()


def load(*arrays):
    return pl.pallas_call(
        load_kernel,
        out_shape=[jax.ShapeDtypeStruct(a.shape, a.dtype) for a in arrays],
        in_specs=anywhere(arrays),
        out_specs=in_vmem(len(arrays)),
        scratch_shapes=[pltpu.SemaphoreType.DMA((len(arrays),))],
        compiler_params=room(44),
        cost_estimate=pl.CostEstimate(
            flops=0, bytes_accessed=2 * sum(a.size * a.dtype.itemsize for a in arrays), transcendentals=0
        ),
        name="load",
    )(*arrays)


def mix_kernel(place_ref, own_ref, other_ref, own_scale_ref, away_scale_ref, *out_refs):
    core, far = place_ref[0], place_ref[1]
    first = core == 0
    for n, half in enumerate((1 - far, far)):
        cut = pl.ds(pl.multiple_of(half * 512 + core * 256, 256), 256)
        scale_ref = away_scale_ref if n == 0 else own_scale_ref
        scales = scale_ref[:, pl.ds(pl.multiple_of(core * 256, 256), 256)]
        guide = 1.0 + 0.5 * scales.astype(jnp.float32)
        own = own_ref[:, cut].astype(jnp.float32)
        other = other_ref[:, cut].astype(jnp.float32)
        cond = jnp.where(first, own, other)
        uncond = jnp.where(first, other, own)
        mixed = uncond + guide * (cond - uncond)
        code = code_of(jnp.max(jnp.abs(mixed), axis=0, keepdims=True))
        out_refs[n][:64] = coded(mixed, scale_of(code))
        out_refs[n][64:] = jnp.broadcast_to(code, (16, 256)).astype(jnp.int32).astype(jnp.int16)


def mix(place, own, other, own_scale, away_scale):
    return pl.pallas_call(
        mix_kernel,
        out_shape=[jax.ShapeDtypeStruct((80, 256), jnp.int16)] * 2,
        in_specs=[pl.BlockSpec(memory_space=pltpu.SMEM)] + in_vmem(4),
        out_specs=in_vmem(2),
        compiler_params=room(4),
        name="mix",
    )(place, own, other, own_scale, away_scale)


def hold_kernel(block_ref, *refs):
    refs[-1][...] = block_ref[...]


def hold(block, after):
    return pl.pallas_call(
        hold_kernel,
        out_shape=jax.ShapeDtypeStruct(block.shape, block.dtype),
        in_specs=in_vmem(1) + anywhere(after),
        out_specs=in_vmem(1)[0],
        compiler_params=room(4),
        name="hold",
    )(block, *after)


def stack_kernel(place_ref, a_ref, b_ref, c_ref, d_ref, *refs):
    out_ref = refs[-1]
    width = a_ref.shape[1]
    row = lax.broadcasted_iota(jnp.int32, (16, width), 0)
    codes = jnp.zeros((16, width), jnp.int32)
    for k, ref in enumerate((a_ref, b_ref, c_ref, d_ref)):
        place = (place_ref[4] - k) & 3
        out_ref[pl.ds(pl.multiple_of(place * 64, 64), 64), :] = ref[:64]
        codes = jnp.where(row & 3 == place, ref[64:].astype(jnp.int32), codes)
    out_ref[256:] = codes.astype(jnp.int16)


def stack(place, parts, after):
    return pl.pallas_call(
        stack_kernel,
        out_shape=jax.ShapeDtypeStruct((272, parts[0].shape[1]), jnp.int16),
        in_specs=[pl.BlockSpec(memory_space=pltpu.SMEM)] + in_vmem(4) + anywhere(after),
        out_specs=in_vmem(1)[0],
        compiler_params=room(4),
        name="stack",
    )(place, *parts, *after)


def pack_kernel(*refs):
    out_ref = refs[-1]
    row = lax.broadcasted_iota(jnp.int32, (16, out_ref.shape[1]), 0)
    codes = jnp.zeros(row.shape, jnp.int32)
    for k in range(4):
        out_ref[256 * k : 256 * k + 256] = refs[k][:256]
        codes = jnp.where(row >> 2 == k, refs[k][256:].astype(jnp.int32), codes)
    out_ref[1024:] = codes.astype(jnp.int16)


def pack(line, after):
    return pl.pallas_call(
        pack_kernel,
        out_shape=jax.ShapeDtypeStruct((1040, line[0].shape[1]), jnp.int16),
        in_specs=in_vmem(4) + anywhere(after),
        out_specs=in_vmem(1)[0],
        compiler_params=room(4),
        name="pack",
    )(*line, *after)


def product_kernel(offsets, adds, place_ref, head_ref, *refs):
    parts, out_ref, total_ref = refs[: len(offsets)], refs[-2], refs[-1]
    core, y, x = place_ref[0], place_ref[2], place_ref[3]
    count = total_ref.shape[0] // 2
    dims = (((0,), (0,)), ((), ()))
    for i, (k, part) in enumerate(zip(offsets, parts)):
        total = None
        scale = scale_of(part[1024:].astype(jnp.float32))
        for piece in range(4):
            high, low = [], []
            for j in range(4):
                at = 4 * piece + j
                values = part[64 * at : 64 * at + 64].astype(jnp.float32) * scale[at : at + 1]
                top = values.astype(jnp.bfloat16)
                high.append(top)
                low.append((values - top.astype(jnp.float32)).astype(jnp.bfloat16))
            both = jnp.concatenate([jnp.concatenate(high, 0), jnp.concatenate(low, 0)], 1)
            row = jnp.where(core == 0, y - k, y - piece) & 3
            column = jnp.where(core == 0, x - piece, x - k) & 3
            weight = head_ref[pl.ds(pl.multiple_of((row * 4 + column) * 256, 256), 256), :]
            term = lax.dot_general(both, weight, dims, preferred_element_type=jnp.float32)
            total = term if total is None else total + term
        if i == 0:
            total_ref[...] = total
        else:
            total_ref[...] += total
    total = total_ref[:count] + total_ref[count:]
    if adds:
        total += refs[len(offsets)][...]
    if out_ref.dtype == jnp.float32:
        out_ref[...] = total
    else:
        code = code_of(jnp.max(jnp.abs(total), axis=1, keepdims=True))
        values = coded(total, scale_of(code))
        half = out_ref.shape[1]
        out_ref[:count] = values[:, :half]
        out_ref[count : 2 * count] = values[:, half:]
        across = jnp.transpose(jnp.broadcast_to(code, (count, 128)))[:16]
        out_ref[2 * count :] = jnp.zeros((16, half), jnp.int16)
        out_ref[2 * count :, :count] = across.astype(jnp.int32).astype(jnp.int16)


def product(place, head, parts, offsets, before=(), send=False, cost=0):
    chosen = [parts[k] for k in offsets]
    tokens, width = chosen[0].shape[1], head.shape[1]
    out = (
        jax.ShapeDtypeStruct((2 * tokens + 16, width // 2), jnp.int16)
        if send
        else jax.ShapeDtypeStruct((tokens, width), jnp.float32)
    )
    return pl.pallas_call(
        functools.partial(product_kernel, offsets, len(before) > 0),
        out_shape=out,
        in_specs=[pl.BlockSpec(memory_space=pltpu.SMEM)] + in_vmem(1 + len(chosen) + len(before)),
        out_specs=in_vmem(1)[0],
        scratch_shapes=[pltpu.VMEM((2 * tokens, width), jnp.float32)],
        compiler_params=room(24),
        cost_estimate=pl.CostEstimate(
            flops=cost * len(offsets) * tokens * 4096 * width, bytes_accessed=0, transcendentals=0
        ),
        name="product",
    )(place, head, *chosen, *before)


def join_kernel(kept_ref, back_ref, guided_ref, stats_ref):
    codes = back_ref[512:, :256].astype(jnp.float32)[:1]
    scale = jnp.transpose(jnp.broadcast_to(scale_of(codes), (128, 256)))[:, :1]
    values = jnp.concatenate([back_ref[:256], back_ref[256:512]], 1)
    guided = kept_ref[...] + values.astype(jnp.float32) * scale
    peak = jnp.max(guided, axis=1, keepdims=True)
    expo = jnp.exp(guided - peak)
    total = jnp.sum(expo, axis=1, keepdims=True)
    moment = jnp.sum(expo * guided, axis=1, keepdims=True)
    lane = lax.broadcasted_iota(jnp.int32, (256, 128), 1)
    table = jnp.transpose(jnp.where(lane == 0, peak + jnp.log(total), moment / total))
    rows = [table[i : i + 1, at : at + 128] for i in (0, 1) for at in (0, 128)]
    stats_ref[...] = jnp.broadcast_to(jnp.concatenate(rows, 0)[None], (64, 4, 128))
    guided_ref[...] = guided


def join(kept, back):
    return pl.pallas_call(
        join_kernel,
        out_shape=(
            jax.ShapeDtypeStruct(kept.shape, jnp.float32),
            jax.ShapeDtypeStruct((64, 4, 128), jnp.float32),
        ),
        in_specs=in_vmem(2),
        out_specs=in_vmem(2),
        compiler_params=room(12),
        name="join",
    )(kept, back)


def local(hidden, head, scale_index, threshold):
    core, far = lax.axis_index("cfg"), lax.axis_index("zh")
    y, x, zl = lax.axis_index("y"), lax.axis_index("x"), lax.axis_index("zl")
    slot = jnp.arange(8)
    place = jnp.zeros((8,), jnp.int32)
    for i, at in enumerate((core, far, y, x, zl)):
        place = jnp.where(slot == i, at, place)
    features = hidden[0].T
    other = lax.ppermute(features, "cfg", [(0, 1), (1, 0)])
    away_scale = lax.ppermute(scale_index, ("zl", "zh"), pairs(("zl", "zh"), nearest_other))
    limits = lax.dynamic_slice_in_dim(threshold, core * 256, 256, 0).astype(jnp.float32) / 8.0

    own, own_scale = load(features, scale_index[None])
    away, home = mix(place, own, other, own_scale, away_scale[None])
    (head,) = load(lax.optimization_barrier((head, away))[0])

    def near(block):
        return [block] + [shifted(block, "zl", k) for k in (1, 2, 3)]

    def spread(block, first, second):
        return [block] + [crossed(block, first, second, k) for k in (1, 2, 3)]

    away_near = near(away)
    away_line = spread(stack(place, away_near, ()), "x", "y")
    away_block = pack(away_line, (head,))
    away_parts = spread(away_block, "y", "x")
    away_sum = product(place, head, away_parts, (0,), cost=1)
    home_near = near(hold(home, away_near[1:]))
    home_line = spread(stack(place, home_near, (away_block, away_sum)), "x", "y")
    away_sum = product(place, head, away_parts, (1, 2), (away_sum,), cost=1)
    sent = product(place, head, away_parts, (3,), (away_sum,), True, cost=1)
    back = lax.ppermute(sent, "zh", [(0, 1), (1, 0)])
    home_parts = spread(pack(home_line, (sent,)), "y", "x")
    kept = product(place, head, home_parts, (0,))
    kept = product(place, head, home_parts, (1, 2), (kept,))
    kept = product(place, head, home_parts, (3,), (kept,))

    guided, stats = join(kept, back)
    stats = lax.all_to_all(stats, ("y", "x", "zl"), 0, 0, tiled=True)
    each, mean = stats[:, :2], stats[:, 2:4]
    top = jnp.max(each, axis=0)
    weight = jnp.exp(each - top)
    total = jnp.sum(weight, axis=0)
    lse = top + jnp.log(total)
    entropy = lse - jnp.sum(weight * mean, axis=0) / total
    lse, entropy = lse.reshape(256), entropy.reshape(256)
    logprob = guided - lse[:, None]
    deviation = -logprob - entropy[:, None]
    typical = jax.nn.sigmoid(2.0 * (limits[:, None] - jnp.abs(deviation)))
    return logprob.astype(jnp.bfloat16), typical.astype(jnp.bfloat16), entropy


def solution(mesh):
    torus = Mesh(mesh.devices.reshape(SIZES), AXES)
    vocab = ("y", "x", "zl")
    return jax.shard_map(
        local,
        mesh=torus,
        in_specs=(P("cfg", None, ("zh", *vocab)), P("zh", vocab), P("zh"), P("zh")),
        out_specs=(P(("zh", "cfg"), vocab), P(("zh", "cfg"), vocab), P(("zh", "cfg"))),
        check_vma=False,
    )
```

```python
import functools
import math

import jax
import jax.numpy as jnp
from jax import lax
from jax.experimental import pallas as pl
from jax.experimental.pallas import tpu as pltpu
from jax.sharding import Mesh, PartitionSpec as P

AXES = ("cfg", "y", "x", "zl", "zh")
SIZES = (2, 4, 4, 4, 2)
TOP = 32767.0
STEP = math.log(2.0) / 256.0


def pairs(axes, move):
    dims = [SIZES[AXES.index(a)] for a in axes]
    route = []
    for i in range(math.prod(dims)):
        rest, at = i, {}
        for a, n in reversed(list(zip(axes, dims))):
            at[a], rest = rest % n, rest // n
        to = move(dict(at))
        j = 0
        for a, n in zip(axes, dims):
            j = j * n + to[a] % n
        route.append((i, j))
    return route


def shifted(block, axis, k):
    return lax.ppermute(block, axis, pairs((axis,), lambda at: {axis: at[axis] + k}))


def crossed(block, first, second, k):
    def move(at):
        along = first if at["cfg"] == 0 else second
        at[along] += k
        return at

    axes = ("cfg", "y", "x")
    return lax.ppermute(block, axes, pairs(axes, move))


def nearest_other(at):
    z = at["zh"] * 4 + at["zl"]
    z = (z + (2 if z % 4 >= 2 else 6)) % 8
    return {"zh": z // 4, "zl": z % 4}


def code_of(largest):
    return jnp.ceil(jnp.log(jnp.maximum(largest, 1e-30)) * (1.0 / STEP)) + 1.0


def scale_of(code):
    return jnp.exp(code * STEP) * (1.0 / TOP)


def coded(values, scale):
    return jnp.clip(jnp.round(values / scale), -TOP, TOP).astype(jnp.int32).astype(jnp.int16)


def in_vmem(count):
    return [pl.BlockSpec(memory_space=pltpu.VMEM)] * count


def anywhere(arrays):
    return [pl.BlockSpec(memory_space=pl.ANY)] * len(arrays)


def room(mib):
    return pltpu.CompilerParams(vmem_limit_bytes=mib << 20)


def load_kernel(*refs):
    count = len(refs) // 2
    copies = [pltpu.make_async_copy(refs[i], refs[count + i], refs[-1].at[i]) for i in range(count)]
    for copy in copies:
        copy.start()
    for copy in copies:
        copy.wait()


def load(*arrays):
    return pl.pallas_call(
        load_kernel,
        out_shape=[jax.ShapeDtypeStruct(a.shape, a.dtype) for a in arrays],
        in_specs=anywhere(arrays),
        out_specs=in_vmem(len(arrays)),
        scratch_shapes=[pltpu.SemaphoreType.DMA((len(arrays),))],
        compiler_params=room(44),
        cost_estimate=pl.CostEstimate(
            flops=0, bytes_accessed=2 * sum(a.size * a.dtype.itemsize for a in arrays), transcendentals=0
        ),
        name="load",
    )(*arrays)


def mix_kernel(place_ref, own_ref, other_ref, own_scale_ref, away_scale_ref, *out_refs):
    core, far = place_ref[0], place_ref[1]
    first = core == 0
    for n, half in enumerate((1 - far, far)):
        cut = pl.ds(pl.multiple_of(half * 512 + core * 256, 256), 256)
        scale_ref = away_scale_ref if n == 0 else own_scale_ref
        scales = scale_ref[:, pl.ds(pl.multiple_of(core * 256, 256), 256)]
        guide = 1.0 + 0.5 * scales.astype(jnp.float32)
        own = own_ref[:, cut].astype(jnp.float32)
        other = other_ref[:, cut].astype(jnp.float32)
        cond = jnp.where(first, own, other)
        uncond = jnp.where(first, other, own)
        mixed = uncond + guide * (cond - uncond)
        code = code_of(jnp.max(jnp.abs(mixed), axis=0, keepdims=True))
        out_refs[n][:64] = coded(mixed, scale_of(code))
        out_refs[n][64:] = jnp.broadcast_to(code, (16, 256)).astype(jnp.int32).astype(jnp.int16)


def mix(place, own, other, own_scale, away_scale):
    return pl.pallas_call(
        mix_kernel,
        out_shape=[jax.ShapeDtypeStruct((80, 256), jnp.int16)] * 2,
        in_specs=[pl.BlockSpec(memory_space=pltpu.SMEM)] + in_vmem(4),
        out_specs=in_vmem(2),
        compiler_params=room(4),
        name="mix",
    )(place, own, other, own_scale, away_scale)


def hold_kernel(block_ref, *refs):
    refs[-1][...] = block_ref[...]


def hold(block, after):
    return pl.pallas_call(
        hold_kernel,
        out_shape=jax.ShapeDtypeStruct(block.shape, block.dtype),
        in_specs=in_vmem(1) + anywhere(after),
        out_specs=in_vmem(1)[0],
        compiler_params=room(4),
        name="hold",
    )(block, *after)


def stack_kernel(place_ref, a_ref, b_ref, c_ref, d_ref, *refs):
    out_ref = refs[-1]
    width = a_ref.shape[1]
    row = lax.broadcasted_iota(jnp.int32, (16, width), 0)
    codes = jnp.zeros((16, width), jnp.int32)
    for k, ref in enumerate((a_ref, b_ref, c_ref, d_ref)):
        place = (place_ref[4] - k) & 3
        out_ref[pl.ds(pl.multiple_of(place * 64, 64), 64), :] = ref[:64]
        codes = jnp.where(row & 3 == place, ref[64:].astype(jnp.int32), codes)
    out_ref[256:] = codes.astype(jnp.int16)


def stack(place, parts, after):
    return pl.pallas_call(
        stack_kernel,
        out_shape=jax.ShapeDtypeStruct((272, parts[0].shape[1]), jnp.int16),
        in_specs=[pl.BlockSpec(memory_space=pltpu.SMEM)] + in_vmem(4) + anywhere(after),
        out_specs=in_vmem(1)[0],
        compiler_params=room(4),
        name="stack",
    )(place, *parts, *after)


def pack_kernel(*refs):
    out_ref = refs[-1]
    row = lax.broadcasted_iota(jnp.int32, (16, out_ref.shape[1]), 0)
    codes = jnp.zeros(row.shape, jnp.int32)
    for k in range(4):
        out_ref[256 * k : 256 * k + 256] = refs[k][:256]
        codes = jnp.where(row >> 2 == k, refs[k][256:].astype(jnp.int32), codes)
    out_ref[1024:] = codes.astype(jnp.int16)


def pack(line, after):
    return pl.pallas_call(
        pack_kernel,
        out_shape=jax.ShapeDtypeStruct((1040, line[0].shape[1]), jnp.int16),
        in_specs=in_vmem(4) + anywhere(after),
        out_specs=in_vmem(1)[0],
        compiler_params=room(4),
        name="pack",
    )(*line, *after)


def product_kernel(offsets, adds, place_ref, head_ref, *refs):
    parts, out_ref, total_ref = refs[: len(offsets)], refs[-2], refs[-1]
    core, y, x = place_ref[0], place_ref[2], place_ref[3]
    count = total_ref.shape[0] // 2
    dims = (((0,), (0,)), ((), ()))
    for i, (k, part) in enumerate(zip(offsets, parts)):
        total = None
        scale = scale_of(part[1024:].astype(jnp.float32))
        for piece in range(4):
            high, low = [], []
            for j in range(4):
                at = 4 * piece + j
                values = part[64 * at : 64 * at + 64].astype(jnp.float32) * scale[at : at + 1]
                top = values.astype(jnp.bfloat16)
                high.append(top)
                low.append((values - top.astype(jnp.float32)).astype(jnp.bfloat16))
            both = jnp.concatenate([jnp.concatenate(high, 0), jnp.concatenate(low, 0)], 1)
            row = jnp.where(core == 0, y - k, y - piece) & 3
            column = jnp.where(core == 0, x - piece, x - k) & 3
            weight = head_ref[pl.ds(pl.multiple_of((row * 4 + column) * 256, 256), 256), :]
            term = lax.dot_general(both, weight, dims, preferred_element_type=jnp.float32)
            total = term if total is None else total + term
        if i == 0:
            total_ref[...] = total
        else:
            total_ref[...] += total
    total = total_ref[:count] + total_ref[count:]
    if adds:
        total += refs[len(offsets)][...]
    if out_ref.dtype == jnp.float32:
        out_ref[...] = total
    else:
        code = code_of(jnp.max(jnp.abs(total), axis=1, keepdims=True))
        values = coded(total, scale_of(code))
        half = out_ref.shape[1]
        out_ref[:count] = values[:, :half]
        out_ref[count : 2 * count] = values[:, half:]
        across = jnp.transpose(jnp.broadcast_to(code, (count, 128)))[:16]
        out_ref[2 * count :] = jnp.zeros((16, half), jnp.int16)
        out_ref[2 * count :, :count] = across.astype(jnp.int32).astype(jnp.int16)


def product(place, head, parts, offsets, before=(), send=False, cost=0):
    chosen = [parts[k] for k in offsets]
    tokens, width = chosen[0].shape[1], head.shape[1]
    out = (
        jax.ShapeDtypeStruct((2 * tokens + 16, width // 2), jnp.int16)
        if send
        else jax.ShapeDtypeStruct((tokens, width), jnp.float32)
    )
    return pl.pallas_call(
        functools.partial(product_kernel, offsets, len(before) > 0),
        out_shape=out,
        in_specs=[pl.BlockSpec(memory_space=pltpu.SMEM)] + in_vmem(1 + len(chosen) + len(before)),
        out_specs=in_vmem(1)[0],
        scratch_shapes=[pltpu.VMEM((2 * tokens, width), jnp.float32)],
        compiler_params=room(24),
        cost_estimate=pl.CostEstimate(
            flops=cost * len(offsets) * tokens * 4096 * width, bytes_accessed=0, transcendentals=0
        ),
        name="product",
    )(place, head, *chosen, *before)


def join_kernel(kept_ref, back_ref, guided_ref, stats_ref):
    codes = back_ref[512:, :256].astype(jnp.float32)[:1]
    scale = jnp.transpose(jnp.broadcast_to(scale_of(codes), (128, 256)))[:, :1]
    values = jnp.concatenate([back_ref[:256], back_ref[256:512]], 1)
    guided = kept_ref[...] + values.astype(jnp.float32) * scale
    peak = jnp.max(guided, axis=1, keepdims=True)
    expo = jnp.exp(guided - peak)
    total = jnp.sum(expo, axis=1, keepdims=True)
    moment = jnp.sum(expo * guided, axis=1, keepdims=True)
    lane = lax.broadcasted_iota(jnp.int32, (256, 128), 1)
    table = jnp.transpose(jnp.where(lane == 0, peak + jnp.log(total), moment / total))
    rows = [table[i : i + 1, at : at + 128] for i in (0, 1) for at in (0, 128)]
    stats_ref[...] = jnp.broadcast_to(jnp.concatenate(rows, 0)[None], (64, 4, 128))
    guided_ref[...] = guided


def join(kept, back):
    return pl.pallas_call(
        join_kernel,
        out_shape=(
            jax.ShapeDtypeStruct(kept.shape, jnp.float32),
            jax.ShapeDtypeStruct((64, 4, 128), jnp.float32),
        ),
        in_specs=in_vmem(2),
        out_specs=in_vmem(2),
        compiler_params=room(12),
        name="join",
    )(kept, back)


def local(hidden, head, scale_index, threshold):
    core, far = lax.axis_index("cfg"), lax.axis_index("zh")
    y, x, zl = lax.axis_index("y"), lax.axis_index("x"), lax.axis_index("zl")
    slot = jnp.arange(8)
    place = jnp.zeros((8,), jnp.int32)
    for i, at in enumerate((core, far, y, x, zl)):
        place = jnp.where(slot == i, at, place)
    features = hidden[0].T
    other = lax.ppermute(features, "cfg", [(0, 1), (1, 0)])
    away_scale = lax.ppermute(scale_index, ("zl", "zh"), pairs(("zl", "zh"), nearest_other))
    limits = lax.dynamic_slice_in_dim(threshold, core * 256, 256, 0).astype(jnp.float32) / 8.0

    own, own_scale = load(features, scale_index[None])
    away, home = mix(place, own, other, own_scale, away_scale[None])
    (head,) = load(lax.optimization_barrier((head, away))[0])

    def near(block):
        return [block] + [shifted(block, "zl", k) for k in (1, 2, 3)]

    def spread(block, first, second):
        return [block] + [crossed(block, first, second, k) for k in (1, 2, 3)]

    away_near = near(away)
    home_near = near(hold(home, away_near[1:]))
    away_line = spread(stack(place, away_near, (head,)), "x", "y")
    away_block = pack(away_line, (home_near[1],))
    away_parts = spread(away_block, "y", "x")
    away_sum = product(place, head, away_parts, (0,), cost=1)
    home_line = spread(stack(place, home_near, (away_block, away_sum)), "x", "y")
    away_sum = product(place, head, away_parts, (1, 2), (away_sum,), cost=1)
    sent = product(place, head, away_parts, (3,), (away_sum,), True, cost=1)
    back = lax.ppermute(sent, "zh", [(0, 1), (1, 0)])
    home_parts = spread(pack(home_line, (sent,)), "y", "x")
    kept = product(place, head, home_parts, (0,))
    kept = product(place, head, home_parts, (1, 2), (kept,))
    kept = product(place, head, home_parts, (3,), (kept,))

    guided, stats = join(kept, back)
    stats = lax.all_to_all(stats, ("y", "x", "zl"), 0, 0, tiled=True)
    each, mean = stats[:, :2], stats[:, 2:4]
    top = jnp.max(each, axis=0)
    weight = jnp.exp(each - top)
    total = jnp.sum(weight, axis=0)
    lse = top + jnp.log(total)
    entropy = lse - jnp.sum(weight * mean, axis=0) / total
    lse, entropy = lse.reshape(256), entropy.reshape(256)
    logprob = guided - lse[:, None]
    deviation = -logprob - entropy[:, None]
    typical = jax.nn.sigmoid(2.0 * (limits[:, None] - jnp.abs(deviation)))
    return logprob.astype(jnp.bfloat16), typical.astype(jnp.bfloat16), entropy


def solution(mesh):
    torus = Mesh(mesh.devices.reshape(SIZES), AXES)
    vocab = ("y", "x", "zl")
    return jax.shard_map(
        local,
        mesh=torus,
        in_specs=(P("cfg", None, ("zh", *vocab)), P("zh", vocab), P("zh"), P("zh")),
        out_specs=(P(("zh", "cfg"), vocab), P(("zh", "cfg"), vocab), P(("zh", "cfg"))),
        check_vma=False,
    )
```

```python
import functools
import math

import jax
import jax.numpy as jnp
from jax import lax
from jax.experimental import pallas as pl
from jax.experimental.pallas import tpu as pltpu
from jax.sharding import Mesh, PartitionSpec as P

AXES = ("cfg", "y", "x", "zl", "zh")
SIZES = (2, 4, 4, 4, 2)
TOP = 32767.0
STEP = math.log(2.0) / 256.0


def pairs(axes, move):
    dims = [SIZES[AXES.index(a)] for a in axes]
    route = []
    for i in range(math.prod(dims)):
        rest, at = i, {}
        for a, n in reversed(list(zip(axes, dims))):
            at[a], rest = rest % n, rest // n
        to = move(dict(at))
        j = 0
        for a, n in zip(axes, dims):
            j = j * n + to[a] % n
        route.append((i, j))
    return route


def shifted(block, axis, k):
    return lax.ppermute(block, axis, pairs((axis,), lambda at: {axis: at[axis] + k}))


def crossed(block, first, second, k):
    def move(at):
        along = first if at["cfg"] == 0 else second
        at[along] += k
        return at

    axes = ("cfg", "y", "x")
    return lax.ppermute(block, axes, pairs(axes, move))


def nearest_other(at):
    z = at["zh"] * 4 + at["zl"]
    z = (z + (2 if z % 4 >= 2 else 6)) % 8
    return {"zh": z // 4, "zl": z % 4}


def code_of(largest):
    return jnp.ceil(jnp.log(jnp.maximum(largest, 1e-30)) * (1.0 / STEP)) + 1.0


def scale_of(code):
    return jnp.exp(code * STEP) * (1.0 / TOP)


def coded(values, scale):
    return jnp.clip(jnp.round(values / scale), -TOP, TOP).astype(jnp.int32).astype(jnp.int16)


def in_vmem(count):
    return [pl.BlockSpec(memory_space=pltpu.VMEM)] * count


def anywhere(arrays):
    return [pl.BlockSpec(memory_space=pl.ANY)] * len(arrays)


def room(mib):
    return pltpu.CompilerParams(vmem_limit_bytes=mib << 20)


def load_kernel(*refs):
    count = len(refs) // 2
    copies = [pltpu.make_async_copy(refs[i], refs[count + i], refs[-1].at[i]) for i in range(count)]
    for copy in copies:
        copy.start()
    for copy in copies:
        copy.wait()


def load(*arrays):
    return pl.pallas_call(
        load_kernel,
        out_shape=[jax.ShapeDtypeStruct(a.shape, a.dtype) for a in arrays],
        in_specs=anywhere(arrays),
        out_specs=in_vmem(len(arrays)),
        scratch_shapes=[pltpu.SemaphoreType.DMA((len(arrays),))],
        compiler_params=room(44),
        cost_estimate=pl.CostEstimate(
            flops=0, bytes_accessed=2 * sum(a.size * a.dtype.itemsize for a in arrays), transcendentals=0
        ),
        name="load",
    )(*arrays)


def mix_kernel(place_ref, own_ref, other_ref, own_scale_ref, away_scale_ref, *out_refs):
    core, far = place_ref[0], place_ref[1]
    first = core == 0
    for n, half in enumerate((1 - far, far)):
        cut = pl.ds(pl.multiple_of(half * 512 + core * 256, 256), 256)
        scale_ref = away_scale_ref if n == 0 else own_scale_ref
        scales = scale_ref[:, pl.ds(pl.multiple_of(core * 256, 256), 256)]
        guide = 1.0 + 0.5 * scales.astype(jnp.float32)
        own = own_ref[:, cut].astype(jnp.float32)
        other = other_ref[:, cut].astype(jnp.float32)
        cond = jnp.where(first, own, other)
        uncond = jnp.where(first, other, own)
        mixed = uncond + guide * (cond - uncond)
        code = code_of(jnp.max(jnp.abs(mixed), axis=0, keepdims=True))
        out_refs[n][:64] = coded(mixed, scale_of(code))
        out_refs[n][64:] = jnp.broadcast_to(code, (16, 256)).astype(jnp.int32).astype(jnp.int16)


def mix(place, own, other, own_scale, away_scale):
    return pl.pallas_call(
        mix_kernel,
        out_shape=[jax.ShapeDtypeStruct((80, 256), jnp.int16)] * 2,
        in_specs=[pl.BlockSpec(memory_space=pltpu.SMEM)] + in_vmem(4),
        out_specs=in_vmem(2),
        compiler_params=room(4),
        name="mix",
    )(place, own, other, own_scale, away_scale)


def hold_kernel(block_ref, *refs):
    refs[-1][...] = block_ref[...]


def hold(block, after):
    return pl.pallas_call(
        hold_kernel,
        out_shape=jax.ShapeDtypeStruct(block.shape, block.dtype),
        in_specs=in_vmem(1) + anywhere(after),
        out_specs=in_vmem(1)[0],
        compiler_params=room(4),
        name="hold",
    )(block, *after)


def stack_kernel(place_ref, a_ref, b_ref, c_ref, d_ref, *refs):
    out_ref = refs[-1]
    width = a_ref.shape[1]
    row = lax.broadcasted_iota(jnp.int32, (16, width), 0)
    codes = jnp.zeros((16, width), jnp.int32)
    for k, ref in enumerate((a_ref, b_ref, c_ref, d_ref)):
        place = (place_ref[4] - k) & 3
        out_ref[pl.ds(pl.multiple_of(place * 64, 64), 64), :] = ref[:64]
        codes = jnp.where(row & 3 == place, ref[64:].astype(jnp.int32), codes)
    out_ref[256:] = codes.astype(jnp.int16)


def stack(place, parts, after):
    return pl.pallas_call(
        stack_kernel,
        out_shape=jax.ShapeDtypeStruct((272, parts[0].shape[1]), jnp.int16),
        in_specs=[pl.BlockSpec(memory_space=pltpu.SMEM)] + in_vmem(4) + anywhere(after),
        out_specs=in_vmem(1)[0],
        compiler_params=room(4),
        name="stack",
    )(place, *parts, *after)


def pack_kernel(*refs):
    out_ref = refs[-1]
    row = lax.broadcasted_iota(jnp.int32, (16, out_ref.shape[1]), 0)
    codes = jnp.zeros(row.shape, jnp.int32)
    for k in range(4):
        out_ref[256 * k : 256 * k + 256] = refs[k][:256]
        codes = jnp.where(row >> 2 == k, refs[k][256:].astype(jnp.int32), codes)
    out_ref[1024:] = codes.astype(jnp.int16)


def pack(line, after):
    return pl.pallas_call(
        pack_kernel,
        out_shape=jax.ShapeDtypeStruct((1040, line[0].shape[1]), jnp.int16),
        in_specs=in_vmem(4) + anywhere(after),
        out_specs=in_vmem(1)[0],
        compiler_params=room(4),
        name="pack",
    )(*line, *after)


def product_kernel(offsets, adds, place_ref, head_ref, *refs):
    parts, out_ref = refs[: len(offsets)], refs[-1]
    core, y, x = place_ref[0], place_ref[2], place_ref[3]
    count = parts[0].shape[1]
    dims = (((0,), (0,)), ((), ()))
    total = refs[len(offsets)][...] if adds else None
    for k, part in zip(offsets, parts):
        scale = scale_of(part[1024:].astype(jnp.float32))
        for piece in range(4):
            high, low = [], []
            for j in range(4):
                at = 4 * piece + j
                values = part[64 * at : 64 * at + 64].astype(jnp.float32) * scale[at : at + 1]
                top = values.astype(jnp.bfloat16)
                high.append(top)
                low.append((values - top.astype(jnp.float32)).astype(jnp.bfloat16))
            row = jnp.where(core == 0, y - k, y - piece) & 3
            column = jnp.where(core == 0, x - piece, x - k) & 3
            weight = head_ref[pl.ds(pl.multiple_of((row * 4 + column) * 256, 256), 256), :]
            for side in (high, low):
                term = lax.dot_general(
                    jnp.concatenate(side, 0), weight, dims, preferred_element_type=jnp.float32
                )
                total = term if total is None else total + term
    if out_ref.dtype == jnp.float32:
        out_ref[...] = total
    else:
        code = code_of(jnp.max(jnp.abs(total), axis=1, keepdims=True))
        values = coded(total, scale_of(code))
        half = out_ref.shape[1]
        out_ref[:count] = values[:, :half]
        out_ref[count : 2 * count] = values[:, half:]
        across = jnp.transpose(jnp.broadcast_to(code, (count, 128)))[:16]
        out_ref[2 * count :] = jnp.zeros((16, half), jnp.int16)
        out_ref[2 * count :, :count] = across.astype(jnp.int32).astype(jnp.int16)


def product(place, head, parts, offsets, before=(), send=False, cost=0):
    chosen = [parts[k] for k in offsets]
    tokens, width = chosen[0].shape[1], head.shape[1]
    out = (
        jax.ShapeDtypeStruct((2 * tokens + 16, width // 2), jnp.int16)
        if send
        else jax.ShapeDtypeStruct((tokens, width), jnp.float32)
    )
    return pl.pallas_call(
        functools.partial(product_kernel, offsets, len(before) > 0),
        out_shape=out,
        in_specs=[pl.BlockSpec(memory_space=pltpu.SMEM)] + in_vmem(1 + len(chosen) + len(before)),
        out_specs=in_vmem(1)[0],
        compiler_params=room(24),
        cost_estimate=pl.CostEstimate(
            flops=cost * len(offsets) * tokens * 4096 * width, bytes_accessed=0, transcendentals=0
        ),
        name="product",
    )(place, head, *chosen, *before)


def join_kernel(kept_ref, back_ref, guided_ref, stats_ref):
    codes = back_ref[512:, :256].astype(jnp.float32)[:1]
    scale = jnp.transpose(jnp.broadcast_to(scale_of(codes), (128, 256)))[:, :1]
    values = jnp.concatenate([back_ref[:256], back_ref[256:512]], 1)
    guided = kept_ref[...] + values.astype(jnp.float32) * scale
    peak = jnp.max(guided, axis=1, keepdims=True)
    expo = jnp.exp(guided - peak)
    total = jnp.sum(expo, axis=1, keepdims=True)
    moment = jnp.sum(expo * guided, axis=1, keepdims=True)
    lane = lax.broadcasted_iota(jnp.int32, (256, 128), 1)
    table = jnp.transpose(jnp.where(lane == 0, peak + jnp.log(total), moment / total))
    rows = [table[i : i + 1, at : at + 128] for i in (0, 1) for at in (0, 128)]
    stats_ref[...] = jnp.broadcast_to(jnp.concatenate(rows, 0)[None], (64, 4, 128))
    guided_ref[...] = guided


def join(kept, back):
    return pl.pallas_call(
        join_kernel,
        out_shape=(
            jax.ShapeDtypeStruct(kept.shape, jnp.float32),
            jax.ShapeDtypeStruct((64, 4, 128), jnp.float32),
        ),
        in_specs=in_vmem(2),
        out_specs=in_vmem(2),
        compiler_params=room(12),
        name="join",
    )(kept, back)


def local(hidden, head, scale_index, threshold):
    core, far = lax.axis_index("cfg"), lax.axis_index("zh")
    y, x, zl = lax.axis_index("y"), lax.axis_index("x"), lax.axis_index("zl")
    slot = jnp.arange(8)
    place = jnp.zeros((8,), jnp.int32)
    for i, at in enumerate((core, far, y, x, zl)):
        place = jnp.where(slot == i, at, place)
    features = hidden[0].T
    other = lax.ppermute(features, "cfg", [(0, 1), (1, 0)])
    away_scale = lax.ppermute(scale_index, ("zl", "zh"), pairs(("zl", "zh"), nearest_other))
    limits = lax.dynamic_slice_in_dim(threshold, core * 256, 256, 0).astype(jnp.float32) / 8.0

    own, own_scale = load(features, scale_index[None])
    away, home = mix(place, own, other, own_scale, away_scale[None])
    (head,) = load(lax.optimization_barrier((head, away))[0])

    def near(block):
        return [block] + [shifted(block, "zl", k) for k in (1, 2, 3)]

    def spread(block, first, second):
        return [block] + [crossed(block, first, second, k) for k in (1, 2, 3)]

    away_near = near(away)
    home_near = near(hold(home, away_near[1:]))
    away_line = spread(stack(place, away_near, (head,)), "x", "y")
    away_block = pack(away_line, (home_near[1],))
    away_parts = spread(away_block, "y", "x")
    away_sum = product(place, head, away_parts, (0,), cost=1)
    home_line = spread(stack(place, home_near, (away_block, away_sum)), "x", "y")
    away_sum = product(place, head, away_parts, (1, 2), (away_sum,), cost=1)
    sent = product(place, head, away_parts, (3,), (away_sum,), True, cost=1)
    back = lax.ppermute(sent, "zh", [(0, 1), (1, 0)])
    home_parts = spread(pack(home_line, (sent,)), "y", "x")
    kept = product(place, head, home_parts, (0,))
    kept = product(place, head, home_parts, (1, 2), (kept,))
    kept = product(place, head, home_parts, (3,), (kept,))

    guided, stats = join(kept, back)
    stats = lax.all_to_all(stats, ("y", "x", "zl"), 0, 0, tiled=True)
    each, mean = stats[:, :2], stats[:, 2:4]
    top = jnp.max(each, axis=0)
    weight = jnp.exp(each - top)
    total = jnp.sum(weight, axis=0)
    lse = top + jnp.log(total)
    entropy = lse - jnp.sum(weight * mean, axis=0) / total
    lse, entropy = lse.reshape(256), entropy.reshape(256)
    logprob = guided - lse[:, None]
    deviation = -logprob - entropy[:, None]
    typical = jax.nn.sigmoid(2.0 * (limits[:, None] - jnp.abs(deviation)))
    return logprob.astype(jnp.bfloat16), typical.astype(jnp.bfloat16), entropy


def solution(mesh):
    torus = Mesh(mesh.devices.reshape(SIZES), AXES)
    vocab = ("y", "x", "zl")
    return jax.shard_map(
        local,
        mesh=torus,
        in_specs=(P("cfg", None, ("zh", *vocab)), P("zh", vocab), P("zh"), P("zh")),
        out_specs=(P(("zh", "cfg"), vocab), P(("zh", "cfg"), vocab), P(("zh", "cfg"))),
        check_vma=False,
    )
```

```python
import functools
import math

import jax
import jax.numpy as jnp
from jax import lax
from jax.experimental import pallas as pl
from jax.experimental.pallas import tpu as pltpu
from jax.sharding import Mesh, PartitionSpec as P

AXES = ("cfg", "y", "x", "zl", "zh")
SIZES = (2, 4, 4, 4, 2)
TOP = 32767.0
STEP = math.log(2.0) / 256.0


def pairs(axes, move):
    dims = [SIZES[AXES.index(a)] for a in axes]
    route = []
    for i in range(math.prod(dims)):
        rest, at = i, {}
        for a, n in reversed(list(zip(axes, dims))):
            at[a], rest = rest % n, rest // n
        to = move(dict(at))
        j = 0
        for a, n in zip(axes, dims):
            j = j * n + to[a] % n
        route.append((i, j))
    return route


def shifted(block, axis, k):
    return lax.ppermute(block, axis, pairs((axis,), lambda at: {axis: at[axis] + k}))


def crossed(block, first, second, k):
    def move(at):
        along = first if at["cfg"] == 0 else second
        at[along] += k
        return at

    axes = ("cfg", "y", "x")
    return lax.ppermute(block, axes, pairs(axes, move))


def nearest_other(at):
    z = at["zh"] * 4 + at["zl"]
    z = (z + (2 if z % 4 >= 2 else 6)) % 8
    return {"zh": z // 4, "zl": z % 4}


def code_of(largest):
    return jnp.ceil(jnp.log(jnp.maximum(largest, 1e-30)) * (1.0 / STEP)) + 1.0


def scale_of(code):
    return jnp.exp(code * STEP) * (1.0 / TOP)


def coded(values, scale):
    return jnp.clip(jnp.round(values / scale), -TOP, TOP).astype(jnp.int32).astype(jnp.int16)


def in_vmem(count):
    return [pl.BlockSpec(memory_space=pltpu.VMEM)] * count


def anywhere(arrays):
    return [pl.BlockSpec(memory_space=pl.ANY)] * len(arrays)


def room(mib):
    return pltpu.CompilerParams(vmem_limit_bytes=mib << 20)


def load_kernel(*refs):
    count = len(refs) // 2
    copies = []
    for i in range(count):
        rows = refs[i].shape[0]
        cuts = 4 if rows >= 4096 else 1
        for j in range(cuts):
            part = pl.ds(j * (rows // cuts), rows // cuts)
            copies.append(
                pltpu.make_async_copy(refs[i].at[part], refs[count + i].at[part], refs[-1].at[4 * i + j])
            )
    for copy in copies:
        copy.start()
    for copy in copies:
        copy.wait()


def load(*arrays):
    return pl.pallas_call(
        load_kernel,
        out_shape=[jax.ShapeDtypeStruct(a.shape, a.dtype) for a in arrays],
        in_specs=anywhere(arrays),
        out_specs=in_vmem(len(arrays)),
        scratch_shapes=[pltpu.SemaphoreType.DMA((4 * len(arrays),))],
        compiler_params=room(44),
        cost_estimate=pl.CostEstimate(
            flops=0, bytes_accessed=2 * sum(a.size * a.dtype.itemsize for a in arrays), transcendentals=0
        ),
        name="load",
    )(*arrays)


def mix_kernel(place_ref, own_ref, other_ref, own_scale_ref, away_scale_ref, *out_refs):
    core, far = place_ref[0], place_ref[1]
    first = core == 0
    for n, half in enumerate((1 - far, far)):
        cut = pl.ds(pl.multiple_of(half * 512 + core * 256, 256), 256)
        scale_ref = away_scale_ref if n == 0 else own_scale_ref
        scales = scale_ref[:, pl.ds(pl.multiple_of(core * 256, 256), 256)]
        guide = 1.0 + 0.5 * scales.astype(jnp.float32)
        own = own_ref[:, cut].astype(jnp.float32)
        other = other_ref[:, cut].astype(jnp.float32)
        cond = jnp.where(first, own, other)
        uncond = jnp.where(first, other, own)
        mixed = uncond + guide * (cond - uncond)
        code = code_of(jnp.max(jnp.abs(mixed), axis=0, keepdims=True))
        out_refs[n][:64] = coded(mixed, scale_of(code))
        out_refs[n][64:] = jnp.broadcast_to(code, (16, 256)).astype(jnp.int32).astype(jnp.int16)


def mix(place, own, other, own_scale, away_scale):
    return pl.pallas_call(
        mix_kernel,
        out_shape=[jax.ShapeDtypeStruct((80, 256), jnp.int16)] * 2,
        in_specs=[pl.BlockSpec(memory_space=pltpu.SMEM)] + in_vmem(4),
        out_specs=in_vmem(2),
        compiler_params=room(4),
        name="mix",
    )(place, own, other, own_scale, away_scale)


def hold_kernel(block_ref, *refs):
    refs[-1][...] = block_ref[...]


def hold(block, after):
    return pl.pallas_call(
        hold_kernel,
        out_shape=jax.ShapeDtypeStruct(block.shape, block.dtype),
        in_specs=in_vmem(1) + anywhere(after),
        out_specs=in_vmem(1)[0],
        compiler_params=room(4),
        name="hold",
    )(block, *after)


def stack_kernel(place_ref, a_ref, b_ref, c_ref, d_ref, *refs):
    out_ref = refs[-1]
    width = a_ref.shape[1]
    row = lax.broadcasted_iota(jnp.int32, (16, width), 0)
    codes = jnp.zeros((16, width), jnp.int32)
    for k, ref in enumerate((a_ref, b_ref, c_ref, d_ref)):
        place = (place_ref[4] - k) & 3
        out_ref[pl.ds(pl.multiple_of(place * 64, 64), 64), :] = ref[:64]
        codes = jnp.where(row & 3 == place, ref[64:].astype(jnp.int32), codes)
    out_ref[256:] = codes.astype(jnp.int16)


def stack(place, parts, after):
    return pl.pallas_call(
        stack_kernel,
        out_shape=jax.ShapeDtypeStruct((272, parts[0].shape[1]), jnp.int16),
        in_specs=[pl.BlockSpec(memory_space=pltpu.SMEM)] + in_vmem(4) + anywhere(after),
        out_specs=in_vmem(1)[0],
        compiler_params=room(4),
        name="stack",
    )(place, *parts, *after)


def pack_kernel(*refs):
    out_ref = refs[-1]
    row = lax.broadcasted_iota(jnp.int32, (16, out_ref.shape[1]), 0)
    codes = jnp.zeros(row.shape, jnp.int32)
    for k in range(4):
        out_ref[256 * k : 256 * k + 256] = refs[k][:256]
        codes = jnp.where(row >> 2 == k, refs[k][256:].astype(jnp.int32), codes)
    out_ref[1024:] = codes.astype(jnp.int16)


def pack(line, after):
    return pl.pallas_call(
        pack_kernel,
        out_shape=jax.ShapeDtypeStruct((1040, line[0].shape[1]), jnp.int16),
        in_specs=in_vmem(4) + anywhere(after),
        out_specs=in_vmem(1)[0],
        compiler_params=room(4),
        name="pack",
    )(*line, *after)


def product_kernel(offsets, adds, place_ref, head_ref, *refs):
    parts, out_ref = refs[: len(offsets)], refs[-1]
    core, y, x = place_ref[0], place_ref[2], place_ref[3]
    count = parts[0].shape[1]
    dims = (((0,), (0,)), ((), ()))
    total = refs[len(offsets)][...] if adds else None
    for k, part in zip(offsets, parts):
        scale = scale_of(part[1024:].astype(jnp.float32))
        for piece in range(4):
            high, low = [], []
            for j in range(4):
                at = 4 * piece + j
                values = part[64 * at : 64 * at + 64].astype(jnp.float32) * scale[at : at + 1]
                top = values.astype(jnp.bfloat16)
                high.append(top)
                low.append((values - top.astype(jnp.float32)).astype(jnp.bfloat16))
            row = jnp.where(core == 0, y - k, y - piece) & 3
            column = jnp.where(core == 0, x - piece, x - k) & 3
            weight = head_ref[pl.ds(pl.multiple_of((row * 4 + column) * 256, 256), 256), :]
            for side in (high, low):
                term = lax.dot_general(
                    jnp.concatenate(side, 0), weight, dims, preferred_element_type=jnp.float32
                )
                total = term if total is None else total + term
    if out_ref.dtype == jnp.float32:
        out_ref[...] = total
    else:
        code = code_of(jnp.max(jnp.abs(total), axis=1, keepdims=True))
        values = coded(total, scale_of(code))
        half = out_ref.shape[1]
        out_ref[:count] = values[:, :half]
        out_ref[count : 2 * count] = values[:, half:]
        across = jnp.transpose(jnp.broadcast_to(code, (count, 128)))[:16]
        out_ref[2 * count :] = jnp.zeros((16, half), jnp.int16)
        out_ref[2 * count :, :count] = across.astype(jnp.int32).astype(jnp.int16)


def product(place, head, parts, offsets, before=(), send=False, cost=0):
    chosen = [parts[k] for k in offsets]
    tokens, width = chosen[0].shape[1], head.shape[1]
    out = (
        jax.ShapeDtypeStruct((2 * tokens + 16, width // 2), jnp.int16)
        if send
        else jax.ShapeDtypeStruct((tokens, width), jnp.float32)
    )
    return pl.pallas_call(
        functools.partial(product_kernel, offsets, len(before) > 0),
        out_shape=out,
        in_specs=[pl.BlockSpec(memory_space=pltpu.SMEM)] + in_vmem(1 + len(chosen) + len(before)),
        out_specs=in_vmem(1)[0],
        compiler_params=room(24),
        cost_estimate=pl.CostEstimate(
            flops=cost * len(offsets) * tokens * 4096 * width, bytes_accessed=0, transcendentals=0
        ),
        name="product",
    )(place, head, *chosen, *before)


def join_kernel(kept_ref, back_ref, guided_ref, stats_ref):
    codes = back_ref[512:, :256].astype(jnp.float32)[:1]
    scale = jnp.transpose(jnp.broadcast_to(scale_of(codes), (128, 256)))[:, :1]
    values = jnp.concatenate([back_ref[:256], back_ref[256:512]], 1)
    guided = kept_ref[...] + values.astype(jnp.float32) * scale
    peak = jnp.max(guided, axis=1, keepdims=True)
    expo = jnp.exp(guided - peak)
    total = jnp.sum(expo, axis=1, keepdims=True)
    moment = jnp.sum(expo * guided, axis=1, keepdims=True)
    lane = lax.broadcasted_iota(jnp.int32, (256, 128), 1)
    table = jnp.transpose(jnp.where(lane == 0, peak + jnp.log(total), moment / total))
    rows = [table[i : i + 1, at : at + 128] for i in (0, 1) for at in (0, 128)]
    stats_ref[...] = jnp.broadcast_to(jnp.concatenate(rows, 0)[None], (64, 4, 128))
    guided_ref[...] = guided


def join(kept, back):
    return pl.pallas_call(
        join_kernel,
        out_shape=(
            jax.ShapeDtypeStruct(kept.shape, jnp.float32),
            jax.ShapeDtypeStruct((64, 4, 128), jnp.float32),
        ),
        in_specs=in_vmem(2),
        out_specs=in_vmem(2),
        compiler_params=room(12),
        name="join",
    )(kept, back)


def local(hidden, head, scale_index, threshold):
    core, far = lax.axis_index("cfg"), lax.axis_index("zh")
    y, x, zl = lax.axis_index("y"), lax.axis_index("x"), lax.axis_index("zl")
    slot = jnp.arange(8)
    place = jnp.zeros((8,), jnp.int32)
    for i, at in enumerate((core, far, y, x, zl)):
        place = jnp.where(slot == i, at, place)
    features = hidden[0].T
    other = lax.ppermute(features, "cfg", [(0, 1), (1, 0)])
    away_scale = lax.ppermute(scale_index, ("zl", "zh"), pairs(("zl", "zh"), nearest_other))
    limits = lax.dynamic_slice_in_dim(threshold, core * 256, 256, 0).astype(jnp.float32) / 8.0

    own, own_scale = load(features, scale_index[None])
    away, home = mix(place, own, other, own_scale, away_scale[None])
    (head,) = load(lax.optimization_barrier((head, away))[0])

    def near(block):
        return [block] + [shifted(block, "zl", k) for k in (1, 2, 3)]

    def spread(block, first, second):
        return [block] + [crossed(block, first, second, k) for k in (1, 2, 3)]

    away_near = near(away)
    home_near = near(hold(home, away_near[1:]))
    away_line = spread(stack(place, away_near, (head,)), "x", "y")
    away_block = pack(away_line, (home_near[1],))
    away_parts = spread(away_block, "y", "x")
    away_sum = product(place, head, away_parts, (0,), cost=1)
    home_line = spread(stack(place, home_near, (away_block, away_sum)), "x", "y")
    away_sum = product(place, head, away_parts, (1, 2), (away_sum,), cost=1)
    sent = product(place, head, away_parts, (3,), (away_sum,), True, cost=1)
    back = lax.ppermute(sent, "zh", [(0, 1), (1, 0)])
    home_parts = spread(pack(home_line, (sent,)), "y", "x")
    kept = product(place, head, home_parts, (0,))
    kept = product(place, head, home_parts, (1, 2), (kept,))
    kept = product(place, head, home_parts, (3,), (kept,))

    guided, stats = join(kept, back)
    stats = lax.all_to_all(stats, ("y", "x", "zl"), 0, 0, tiled=True)
    each, mean = stats[:, :2], stats[:, 2:4]
    top = jnp.max(each, axis=0)
    weight = jnp.exp(each - top)
    total = jnp.sum(weight, axis=0)
    lse = top + jnp.log(total)
    entropy = lse - jnp.sum(weight * mean, axis=0) / total
    lse, entropy = lse.reshape(256), entropy.reshape(256)
    logprob = guided - lse[:, None]
    deviation = -logprob - entropy[:, None]
    typical = jax.nn.sigmoid(2.0 * (limits[:, None] - jnp.abs(deviation)))
    return logprob.astype(jnp.bfloat16), typical.astype(jnp.bfloat16), entropy


def solution(mesh):
    torus = Mesh(mesh.devices.reshape(SIZES), AXES)
    vocab = ("y", "x", "zl")
    return jax.shard_map(
        local,
        mesh=torus,
        in_specs=(P("cfg", None, ("zh", *vocab)), P("zh", vocab), P("zh"), P("zh")),
        out_specs=(P(("zh", "cfg"), vocab), P(("zh", "cfg"), vocab), P(("zh", "cfg"))),
        check_vma=False,
    )
```
